256 devices in a mesh: half: 4 (over z_lo, core), gz: 64 (over x, y, z_hi).
Axes of the slice: x: 4, y: 4, z: 8 (z_hi: 4, z_lo: 2; z = z_hi * 2 + z_lo), core: 2. Of those that a mesh axis runs over, the one named last changes fastest.
Arguments:
- density: float32 [4, 256, 4, 2048], P('half', 'gz'), may hold values from -6 to 6
- lift_weight: float32 [16], replicated, may hold values from -3 to 3
- lift_bias: float32 [16], replicated, may hold values from -1 to 1
- conv_first: bfloat16 [16, 16, 3, 3, 3], replicated, may hold values from -0.3125 to 0.3125
- bias_first: float32 [16], replicated, may hold values from -1 to 1
- conv_second: bfloat16 [16, 16, 3, 3, 3], replicated, may hold values from -0.3125 to 0.3125
- bias_second: float32 [16], replicated, may hold values from -1 to 1
- projection: float32 [16], replicated, may hold values from -1.5 to 1.5
- wedge: float32 [256, 2048], replicated, may hold values from 0.1 to 1
Outputs:
- residual: float32 [4, 256, 4, 2048], P('half', 'gz')
The draws below stay inside these ranges and needn't reach their ends.
All inputs are finite; a program needn't handle non-finite values.
Results may differ from the reference program's by a relative error of at most 0.04.
Values may be sent and summed in bfloat16 or wider, within the bound.
No kernel may reach another device: no remote copies, remote signals or barrier semaphores. Data moves between devices by JAX's collectives and lax.ppermute only.
A program may use at most 128 MiB of HBM per device.

```python
import math
import jax
import jax.numpy as jnp
from jax import lax

NX = 2048
CH = 16
NY = 4
NZ = 256
GROUPS = 4


def block_scale(key, dims, split, smallest, top_value):
    gain = 1.0
    for axis_at, shards_of in split:
        draws = jax.random.uniform(jax.random.fold_in(jax.random.fold_in(key, 6), axis_at), (shards_of,), jnp.float32, smallest / len(split), top_value / len(split))
        gain = gain * jnp.repeat(jnp.exp(draws), dims[axis_at] // shards_of).reshape((-1,) + (1,) * (len(dims) - 1 - axis_at))
    return gain


def gaussian(rng, extent, width, limit, split=(), kind=jnp.bfloat16):
    entries = width * jax.random.normal(rng, extent, jnp.float32)
    if split:
        entries = entries * block_scale(rng, extent, split, -0.22, 0.18)
    return jnp.clip(entries, -limit, limit).astype(kind)


def setup_inputs(seed: int = 0) -> dict:
    seeds = jax.random.split(jax.random.key(seed), 10)
    density = gaussian(seeds[0], (GROUPS, NZ, NY, NX), 1.0, 6.0, ((0, 4), (1, 64)), jnp.float32)
    lift_weight = gaussian(seeds[1], (CH,), 1.0, 3.0, (), jnp.float32)
    lift_bias = jnp.clip(jax.random.uniform(seeds[2], (CH,), jnp.float32, -1.0, 1.0), -1.0, 1.0)
    conv_first = gaussian(seeds[3], (CH, CH, 3, 3, 3), (27 * CH) ** -0.5, 0.3125)
    bias_first = jnp.clip(jax.random.uniform(seeds[4], (CH,), jnp.float32, -1.0, 1.0), -1.0, 1.0)
    conv_second = gaussian(seeds[5], (CH, CH, 3, 3, 3), (27 * CH) ** -0.5, 0.3125)
    bias_second = jnp.clip(jax.random.uniform(seeds[6], (CH,), jnp.float32, -1.0, 1.0), -1.0, 1.0)
    projection = gaussian(seeds[7], (CH,), CH ** -0.5, 1.5, (), jnp.float32)
    wedge = jnp.clip(jax.random.uniform(seeds[8], (NZ, NX), jnp.float32, 0.1, 1.0), 0.1, 1.0)
    return {"density": density, "lift_weight": lift_weight, "lift_bias": lift_bias, "conv_first": conv_first, "bias_first": bias_first, "conv_second": conv_second, "bias_second": bias_second, "projection": projection, "wedge": wedge}


def tables(count, first, size):
    rows_idx = jnp.arange(size, dtype=jnp.int32)[:, None]
    cols_idx = first + jnp.arange(count, dtype=jnp.int32)[None, :]
    product = (rows_idx * cols_idx) % size
    angle = product.astype(jnp.float32) * (2.0 * math.pi / size)
    return jnp.cos(angle).astype(jnp.bfloat16), jnp.sin(angle).astype(jnp.bfloat16)


def convolve(feat, kernel):
    out = lax.conv_general_dilated(feat[None], kernel, (1, 1, 1), ((1, 1), (1, 1), (1, 1)), dimension_numbers=("NCDHW", "OIDHW", "NCDHW"), preferred_element_type=jnp.float32)
    return out[0]


def weigh_group(volume, lift_weight, lift_bias, conv_first, bias_first, conv_second, bias_second, projection, wedge):
    lifted = jax.nn.silu(lift_weight[:, None, None, None] * volume[None] + lift_bias[:, None, None, None]).astype(jnp.bfloat16)
    first = jax.nn.silu(convolve(lifted, conv_first) + bias_first[:, None, None, None]).astype(jnp.bfloat16)
    second = jax.nn.silu(convolve(first, conv_second) + bias_second[:, None, None, None])
    mixed = (volume + jnp.einsum("c,czyx->zyx", projection, second)).astype(jnp.bfloat16)
    cos_x, sin_x = tables(NX, 0, NX)
    cos_z, sin_z = tables(NZ, 0, NZ)
    flat = mixed.reshape(NZ * NY, NX)
    spec_re = jnp.dot(flat, cos_x, preferred_element_type=jnp.float32).astype(jnp.bfloat16).reshape(NZ, NY * NX)
    spec_im = (-jnp.dot(flat, sin_x, preferred_element_type=jnp.float32)).astype(jnp.bfloat16).reshape(NZ, NY * NX)
    freq_re = jnp.dot(cos_z, spec_re, preferred_element_type=jnp.float32) + jnp.dot(sin_z, spec_im, preferred_element_type=jnp.float32)
    freq_im = jnp.dot(cos_z, spec_im, preferred_element_type=jnp.float32) - jnp.dot(sin_z, spec_re, preferred_element_type=jnp.float32)
    weights = jnp.tile(wedge, (1, NY))
    weighted_re = (freq_re * weights).astype(jnp.bfloat16)
    weighted_im = (freq_im * weights).astype(jnp.bfloat16)
    return weighted_re, weighted_im


def invert_group(diff_re, diff_im):
    cos_x, sin_x = tables(NX, 0, NX)
    cos_z, sin_z = tables(NZ, 0, NZ)
    back_re = (jnp.dot(cos_z, diff_re, preferred_element_type=jnp.float32) - jnp.dot(sin_z, diff_im, preferred_element_type=jnp.float32)).astype(jnp.bfloat16)
    back_im = (jnp.dot(cos_z, diff_im, preferred_element_type=jnp.float32) + jnp.dot(sin_z, diff_re, preferred_element_type=jnp.float32)).astype(jnp.bfloat16)
    back_re = back_re.reshape(NZ * NY, NX)
    back_im = back_im.reshape(NZ * NY, NX)
    result = jnp.dot(back_re, cos_x, preferred_element_type=jnp.float32) - jnp.dot(back_im, sin_x, preferred_element_type=jnp.float32)
    result = result * (1.0 / (NX * NZ))
    return result.reshape(NZ, NY, NX)


def reference(density, lift_weight, lift_bias, conv_first, bias_first, conv_second, bias_second, projection, wedge):
    spectra = []
    for group in range(GROUPS):
        spectra.append(weigh_group(density[group], lift_weight, lift_bias, conv_first, bias_first, conv_second, bias_second, projection, wedge))
    results = []
    for group in range(GROUPS):
        own_re, own_im = spectra[group]
        other_re, other_im = spectra[group ^ 1]
        diff_re = (own_re.astype(jnp.float32) - other_re.astype(jnp.float32)).astype(jnp.bfloat16)
        diff_im = (own_im.astype(jnp.float32) - other_im.astype(jnp.float32)).astype(jnp.bfloat16)
        results.append(invert_group(diff_re, diff_im))
    return jnp.stack(results)
```

```python
import math

import jax
import jax.numpy as jnp
import numpy as np
from jax import lax
from jax.experimental import pallas as pl
from jax.experimental.pallas import tpu as pltpu
from jax.sharding import PartitionSpec as P

NX, CH, NY, NZ = 2048, 16, 4, 256
GZ = 64
DEPTH = NZ // GZ
RADIX, INNER = 16, NX // 16
HALF = INNER // 2
BLOCKS = 16
LAG = 2
F32, BF16 = jnp.float32, jnp.bfloat16


def dot(a, b):
    return jnp.dot(a, b, preferred_element_type=F32)


def params(megabytes=8):
    return pltpu.CompilerParams(vmem_limit_bytes=megabytes << 20)


def turn(product, size):
    angle = 2.0 * math.pi * (product % size) / size
    return np.cos(angle), np.sin(angle)


def x_tables():
    x0 = np.arange(INNER)[:, None]
    k0 = np.arange(INNER)[None, :]
    c, s = turn(x0 * k0, INNER)
    pick = lambda t, h: t[:, h * HALF : (h + 1) * HALF]
    from_re = np.concatenate([pick(c, 0), pick(-s, 0), pick(c, 1), pick(-s, 1)], 1)
    from_im = np.concatenate([pick(s, 0), pick(c, 0), pick(s, 1), pick(c, 1)], 1)
    full = np.concatenate([from_re, from_im], 0)
    first = np.concatenate([pick(c, 0), pick(-s, 0)], 1)
    first[:, HALF] = c[:, HALF]
    c8, s8 = turn(x0 * (1 + 2 * np.arange(HALF)[None, :]), 2 * INNER)
    middle = np.concatenate([c8, -s8], 1)
    k1 = np.arange(1, 8)[:, None]
    ct, st = turn(k1 * np.arange(INNER)[None, :], NX)
    twiddle = np.concatenate([ct, np.zeros((1, INNER)), st, np.zeros((1, INNER))], 0)
    return (
        full.astype(jnp.bfloat16),
        np.concatenate([first, middle], 1).astype(jnp.bfloat16),
        full.T.astype(jnp.bfloat16),
        np.concatenate([first.T, middle.T], 1).astype(jnp.bfloat16),
        twiddle.astype(np.float32),
    )


def z_tables():
    kz = np.arange(NZ)[:, None]
    row = np.arange(NZ)[None, :]
    ahead = np.concatenate(turn(kz * (row - LAG), NZ), 0)
    back = np.concatenate(turn(kz * row, NZ), 0)
    return ahead.astype(jnp.bfloat16), back.astype(jnp.bfloat16)


def weights_kernel(edge_ref, first_ref, second_ref, w1_ref, w1m_ref, w2a_ref, w2b_ref):
    rows = lax.broadcasted_iota(jnp.int32, (128, 256), 0)
    cols = lax.broadcasted_iota(jnp.int32, (128, 256), 1)
    zo, yo = rows // 64, rows % 4
    zi, yi = cols // 64, cols % 4
    inner = edge_ref[0] == 0
    keep_mid = ((zi >= 2) == (zo == 1)) | inner
    keep_low = (zi <= 2) | inner
    keep_high = (zi >= 1) | inner
    spread_rows = (
        lax.broadcasted_iota(jnp.int32, (128, CH), 0) % 64 // 4
        == lax.broadcasted_iota(jnp.int32, (128, CH), 1)
    ).astype(F32).astype(BF16)
    spread_cols = (
        lax.broadcasted_iota(jnp.int32, (CH, 256), 1) % 64 // 4
        == lax.broadcasted_iota(jnp.int32, (CH, 256), 0)
    ).astype(F32).astype(BF16)
    place = (zi - zo) * 3 + (yi - yo + 1)
    valid = (yi - yo + 1 >= 0) & (yi - yo + 1 <= 2) & (zi - zo >= 0) & (zi - zo <= 2)
    place = jnp.where(valid, place, -1)
    for src, outs in (
        (first_ref, ((w1_ref, None), (w1m_ref, keep_mid))),
        (second_ref, ((w2a_ref, keep_low), (w2b_ref, keep_high))),
    ):
        wide = dot(src[...], spread_cols).astype(BF16)
        for e in range(3):
            total = jnp.zeros((128, 256), F32)
            for ab in range(9):
                at = (e * 9 + ab) * CH
                total = jnp.where(place == ab, dot(spread_rows, wide[at : at + CH]), total)
            total = total * 0.5
            for out, keep in outs:
                part = total if keep is None else jnp.where(keep, total, 0.0)
                out[:, e * 256 : (e + 1) * 256] = part.astype(BF16)


def silu_of_half(h):
    return h + h * jnp.tanh(h)


def filter_kernel(
    left_ref, own_ref, par_ref, w1_ref, w1m_ref, w2a_ref, w2b_ref, out_ref, x1, x2
):
    lane = lax.broadcasted_iota(jnp.int32, (16, NX), 1)
    at_start, at_end = lane == 0, lane == NX - 1

    def spread(ref, row, value):
        rows = pl.ds(row, 16)
        wide = value.astype(F32)
        ref[1, rows, :] = value
        ref[0, rows, :] = jnp.where(at_start, 0.0, pltpu.roll(wide, 1, 1)).astype(BF16)
        ref[2, rows, :] = jnp.where(at_end, 0.0, pltpu.roll(wide, NX - 1, 1)).astype(BF16)

    for z in range(2 * DEPTH):
        cells = left_ref[z] if z < DEPTH else own_ref[z - DEPTH]
        cells = jnp.concatenate([cells] * 4, axis=0)
        for block in range(4):
            gain = par_ref[block * 16 : block * 16 + 16, 0:1]
            shift = par_ref[block * 16 : block * 16 + 16, 1:2]
            lifted = silu_of_half(gain * cells + shift).astype(BF16)
            spread(x1, z * 64 + block * 16, lifted)

    chunk = 256

    def three(w_ref, x_ref, row, at):
        total = None
        for e in range(3):
            part = dot(w_ref[:, e * 256 : (e + 1) * 256], x_ref[e, row : row + 256, pl.ds(at, chunk)])
            total = part if total is None else total + part
        return total

    bias1 = par_ref[:, 2:3]
    bias1 = jnp.concatenate([bias1, bias1], 0)

    @pl.loop(0, NX // chunk)
    def _(index):
        at = pl.multiple_of(index * chunk, chunk)
        for g, w_ref in enumerate((w1_ref, w1m_ref, w1_ref)):
            pre = three(w_ref, x1, 128 * g, at) + bias1
            x2[1, 128 * g : 128 * g + 128, pl.ds(at, chunk)] = silu_of_half(pre).astype(BF16)

    @pl.loop(0, 24)
    def _(index):
        row = pl.multiple_of(index * 16, 16)
        spread(x2, row, x2[1, pl.ds(row, 16), :])

    bias2 = par_ref[:, 3:4]
    bias2 = jnp.concatenate([bias2, bias2], 0)
    mix = par_ref[:, 4:5]

    @pl.loop(0, NX // chunk)
    def _(index):
        at = pl.multiple_of(index * chunk, chunk)
        slices = []
        for g, w_ref in enumerate((w2a_ref, w2b_ref)):
            act = silu_of_half(three(w_ref, x2, 128 * g, at) + bias2)
            for zo in range(2):
                terms = act[zo * 64 : zo * 64 + 64] * mix
                total = terms[0:8]
                for pair in range(1, 8):
                    total = total + terms[pair * 8 : pair * 8 + 8]
                z = 2 + 2 * g + zo
                base = left_ref[z, :, pl.ds(at, chunk)] if z < DEPTH else own_ref[z - DEPTH, :, pl.ds(at, chunk)]
                slices.append(base + total[0:4] + total[4:8])
        mixed = jnp.concatenate([slices[z][y : y + 1] for y in range(NY) for z in range(DEPTH)], 0)
        out_ref[:, pl.ds(at, chunk)] = mixed.astype(BF16)


def cos16(n):
    return math.cos(2 * math.pi * (n % 16) / 16)


def sin16(n):
    return math.sin(2 * math.pi * (n % 16) / 16)


def weigh(terms):
    total = None
    for factor, value in terms:
        if abs(factor) < 1e-9:
            continue
        if abs(factor - 1) < 1e-9:
            term = value
        elif abs(factor + 1) < 1e-9:
            term = -value
        else:
            term = value * factor
        total = term if total is None else total + term
    return total


def forward_kernel(own_ref, other_ref, full_ref, ends_ref, twiddle_ref, out_ref):
    delta = own_ref[...].astype(F32) - other_ref[...].astype(F32)
    a = [delta[:, INNER * i : INNER * (i + 1)] for i in range(RADIX)]
    plus = [a[i] + a[16 - i] for i in range(1, 8)]
    minus = [a[i] - a[16 - i] for i in range(1, 8)]
    re, im = [], []
    for k1 in range(9):
        re.append(weigh([(1, a[0]), ((-1) ** k1, a[8])] + [(cos16(k1 * i), plus[i - 1]) for i in range(1, 8)]))
        im.append(weigh([(-sin16(k1 * i), minus[i - 1]) for i in range(1, 8)]))
    rows = []
    for k1 in range(1, 8):
        c, s = twiddle_ref[k1 - 1 : k1], twiddle_ref[k1 + 7 : k1 + 8]
        rows.append(jnp.concatenate([re[k1] * c + im[k1] * s, im[k1] * c - re[k1] * s], 1))
    whole = dot(jnp.concatenate(rows, 0).astype(BF16), full_ref[...])
    blocks = [
        dot(re[0].astype(BF16), ends_ref[:, :INNER]),
        dot(re[8].astype(BF16), ends_ref[:, INNER:]),
    ]
    for k1 in range(1, 8):
        for h in range(2):
            blocks.append(whole[(k1 - 1) * 16 : k1 * 16, h * INNER : (h + 1) * INNER])
    for y in range(NY):
        for b in range(BLOCKS):
            out_ref[y * BLOCKS + b] = blocks[b][y * DEPTH : (y + 1) * DEPTH].astype(BF16)


def inverse_kernel(in_ref, full_ref, ends_ref, twiddle_ref, out_ref):
    blocks = [
        jnp.concatenate([in_ref[y * BLOCKS + b].astype(F32) for y in range(NY)], 0).astype(BF16)
        for b in range(BLOCKS)
    ]
    even = dot(blocks[0], ends_ref[:, :INNER])
    mid = dot(blocks[1], ends_ref[:, INNER:])
    lows = jnp.concatenate([blocks[2 * k1] for k1 in range(1, 8)], 0)
    highs = jnp.concatenate([blocks[2 * k1 + 1] for k1 in range(1, 8)], 0)
    whole = dot(lows, full_ref[:INNER]) + dot(highs, full_ref[INNER:])
    re, im = [], []
    for k1 in range(1, 8):
        part = whole[(k1 - 1) * 16 : k1 * 16]
        b_re, b_im = part[:, :INNER], part[:, INNER:]
        c, s = twiddle_ref[k1 - 1 : k1], twiddle_ref[k1 + 7 : k1 + 8]
        re.append(b_re * c - b_im * s)
        im.append(b_re * s + b_im * c)
    scale = 1.0 / (NX * NZ)
    even, mid = even * scale, mid * scale
    re, im = [v * scale for v in re], [v * scale for v in im]
    out = [None] * RADIX
    for x1 in range(9):
        p = weigh([(1, even), ((-1) ** x1, mid)] + [(cos16(k1 * x1), re[k1 - 1]) for k1 in range(1, 8)])
        q = weigh([(sin16(k1 * x1), im[k1 - 1]) for k1 in range(1, 8)])
        if q is None:
            out[x1] = p
        else:
            out[x1], out[16 - x1] = p - q, p + q
    for x1 in range(RADIX):
        for z in range(DEPTH):
            rows = [out[x1][y * DEPTH + z : y * DEPTH + z + 1] for y in range(NY)]
            out_ref[z, :, x1 * INNER : (x1 + 1) * INNER] = jnp.concatenate(rows, 0)


def wedge_kernel(at_ref, wedge_ref, plus_ref, minus_ref):
    block = at_ref[0]
    k = lax.broadcasted_iota(jnp.int32, (NX, INNER), 0)
    j = lax.broadcasted_iota(jnp.int32, (NX, INNER), 1)
    col = j % HALF
    k1 = jnp.where(block == 0, 0, jnp.where(block == 1, 8, block // 2))
    high = jnp.where(block < 2, 0, block % 2)
    mine = k1 + RADIX * (HALF * high + col)
    target = jnp.where(j < HALF, mine, (NX - mine) % NX)
    special = (block == 0) & (col == 0)
    quarter = special & (k == NX // 2)
    hit = (k == target)
    plain = jnp.where(hit, jnp.where(special, 0.25, 1.0), 0.0) + jnp.where(quarter, 0.25, 0.0)
    cross = jnp.where(special, jnp.where(hit, 0.25, 0.0) - jnp.where(quarter, 0.25, 0.0), 0.0)
    select = jnp.concatenate([plain, cross], 1).astype(BF16)
    whole = wedge_ref[...]
    top = whole.astype(BF16)
    rest = (whole - top.astype(F32)).astype(BF16)
    picked = dot(top, select) + dot(rest, select)
    r = lax.broadcasted_iota(jnp.int32, (NZ, NZ), 0)
    c = lax.broadcasted_iota(jnp.int32, (NZ, NZ), 1)
    flip = ((r + c) % NZ == 0).astype(F32).astype(BF16)
    top = picked.astype(BF16)
    rest = (picked - top.astype(F32)).astype(BF16)
    turned = dot(flip, top) + dot(flip, rest)
    low = lax.broadcasted_iota(jnp.int32, (NZ, INNER), 1) < HALF
    for out, at in ((plus_ref, 0), (minus_ref, INNER)):
        here, there = picked[:, at : at + INNER], turned[:, at : at + INNER]
        both = jnp.where(low, here + pltpu.roll(there, HALF, 1), there + pltpu.roll(here, HALF, 1))
        out[...] = both


def middle_kernel(in_ref, plus_ref, minus_ref, ahead_ref, back_ref, out_ref):
    sign = jnp.where(lax.broadcasted_iota(jnp.int32, (NZ, INNER), 1) < HALF, 1.0, -1.0)
    both = dot(ahead_ref[...], in_ref[...])
    cos_part, sin_part = both[:NZ], pltpu.roll(both[NZ:], HALF, 1)
    freq = cos_part + sign * sin_part
    mirror = sign * cos_part - sin_part
    weighted = (plus_ref[...] * freq + minus_ref[...] * mirror).astype(BF16)
    both = dot(back_ref[...], weighted)
    out_ref[...] = (both[:NZ] - sign * pltpu.roll(both[NZ:], HALF, 1)).astype(BF16)


def call(kernel, outs, *args, scratch=(), megabytes=8, smem=0, flops=10**7):
    many = isinstance(outs, list)
    vmem = pl.BlockSpec(memory_space=pltpu.VMEM)
    scalar = pl.BlockSpec(memory_space=pltpu.SMEM)
    moved = sum(a.size * a.dtype.itemsize for a in args)
    return pl.pallas_call(
        kernel,
        out_shape=outs,
        in_specs=[scalar] * smem + [vmem] * (len(args) - smem),
        out_specs=[vmem] * len(outs) if many else vmem,
        scratch_shapes=scratch,
        compiler_params=params(megabytes),
        cost_estimate=pl.CostEstimate(flops=flops, bytes_accessed=moved, transcendentals=0),
    )(*args)


def shape(*dims, dtype=BF16):
    return jax.ShapeDtypeStruct(dims, dtype)


def body(
    density,
    lift_weight,
    lift_bias,
    conv_first,
    bias_first,
    conv_second,
    bias_second,
    projection,
    wedge,
):
    full_x, ends_x, full_i, ends_i, twiddle = x_tables()
    ahead, back = z_tables()
    place = lax.axis_index("gz")
    slab = density[0]
    left = lax.ppermute(slab, "gz", [(i, (i + 1) % GZ) for i in range(GZ)])

    edge = (place == 0).astype(jnp.int32).reshape(1)
    block = (place % BLOCKS).astype(jnp.int32).reshape(1)
    flat = lambda w: w.transpose(4, 2, 3, 0, 1).reshape(27 * CH, CH)
    weights = call(
        weights_kernel, [shape(128, 768)] * 4, edge, flat(conv_first), flat(conv_second),
        smem=1, megabytes=16, flops=10**9,
    )
    plus, minus = call(
        wedge_kernel, [shape(NZ, INNER, dtype=F32)] * 2, block, wedge,
        smem=1, megabytes=32, flops=10**9,
    )
    columns = jnp.stack(
        [0.5 * lift_weight, 0.5 * lift_bias, 0.5 * bias_first, 0.5 * bias_second, projection], 1
    )
    columns = jnp.repeat(columns, NY, axis=0)

    mixed = call(
        filter_kernel, shape(NY * DEPTH, NX), left, slab, columns, *weights,
        scratch=[pltpu.VMEM((3, 512, NX), BF16), pltpu.VMEM((3, 384, NX), BF16)],
        megabytes=40, flops=10**10,
    )
    other = lax.ppermute(mixed, "half", [(i, i ^ 1) for i in range(lax.axis_size("half"))])
    spectrum = call(
        forward_kernel, shape(GZ, DEPTH, INNER), mixed, other, full_x, ends_x, twiddle,
    )
    pencils = lax.all_to_all(spectrum, "gz", split_axis=0, concat_axis=0, tiled=True)
    returned = call(
        middle_kernel, shape(NZ, INNER), pencils.reshape(NZ, INNER), plus, minus, ahead, back,
    )
    slabs = lax.all_to_all(
        returned.reshape(GZ, DEPTH, INNER), "gz", split_axis=0, concat_axis=0, tiled=True
    )
    residual = call(
        inverse_kernel, shape(DEPTH, NY, NX, dtype=F32), slabs, full_i, ends_i, twiddle,
    )
    return residual[None]


def solution(mesh):
    placed = (P("half", "gz", None, None), P(), P(), P(), P(), P(), P(), P(), P())
    return jax.shard_map(
        body, mesh=mesh, in_specs=placed, out_specs=P("half", "gz", None, None), check_vma=False
    )
```

```python
import math

import jax
import jax.numpy as jnp
import numpy as np
from jax import lax
from jax.experimental import pallas as pl
from jax.experimental.pallas import tpu as pltpu
from jax.sharding import PartitionSpec as P

NX, CH, NY, NZ = 2048, 16, 4, 256
GZ = 64
DEPTH = NZ // GZ
RADIX, INNER = 16, NX // 16
HALF = INNER // 2
BLOCKS = 16
LAG = 2
F32, BF16 = jnp.float32, jnp.bfloat16


def dot(a, b):
    return jnp.dot(a, b, preferred_element_type=F32)


def params(megabytes=8):
    return pltpu.CompilerParams(vmem_limit_bytes=megabytes << 20)


def turn(product, size):
    angle = 2.0 * math.pi * (product % size) / size
    return np.cos(angle), np.sin(angle)


def x_tables():
    x0 = np.arange(INNER)[:, None]
    k0 = np.arange(INNER)[None, :]
    c, s = turn(x0 * k0, INNER)
    pick = lambda t, h: t[:, h * HALF : (h + 1) * HALF]
    from_re = np.concatenate([pick(c, 0), pick(-s, 0), pick(c, 1), pick(-s, 1)], 1)
    from_im = np.concatenate([pick(s, 0), pick(c, 0), pick(s, 1), pick(c, 1)], 1)
    full = np.concatenate([from_re, from_im], 0)
    first = np.concatenate([pick(c, 0), pick(-s, 0)], 1)
    first[:, HALF] = c[:, HALF]
    c8, s8 = turn(x0 * (1 + 2 * np.arange(HALF)[None, :]), 2 * INNER)
    middle = np.concatenate([c8, -s8], 1)
    k1 = np.arange(1, 8)[:, None]
    ct, st = turn(k1 * np.arange(INNER)[None, :], NX)
    twiddle = np.concatenate([ct, np.zeros((1, INNER)), st, np.zeros((1, INNER))], 0)
    return (
        full.astype(jnp.bfloat16),
        np.concatenate([first, middle], 1).astype(jnp.bfloat16),
        full.T.astype(jnp.bfloat16),
        np.concatenate([first.T, middle.T], 1).astype(jnp.bfloat16),
        twiddle.astype(np.float32),
    )


def z_tables():
    kz = np.arange(NZ)[:, None]
    row = np.arange(NZ)[None, :]
    ahead = np.concatenate(turn(kz * (row - LAG), NZ), 0)
    back = np.concatenate(turn(kz * row, NZ), 0)
    return ahead.astype(jnp.bfloat16), back.astype(jnp.bfloat16)


def build_weights(inner, conv, outs):
    rows = lax.broadcasted_iota(jnp.int32, (128, 256), 0)
    cols = lax.broadcasted_iota(jnp.int32, (128, 256), 1)
    zo, yo = rows // 64, rows % 4
    zi, yi = cols // 64, cols % 4
    spread_rows = (
        lax.broadcasted_iota(jnp.int32, (128, CH), 0) % 64 // 4
        == lax.broadcasted_iota(jnp.int32, (128, CH), 1)
    ).astype(F32).astype(BF16)
    spread_cols = (
        lax.broadcasted_iota(jnp.int32, (CH, 256), 1) % 64 // 4
        == lax.broadcasted_iota(jnp.int32, (CH, 256), 0)
    ).astype(F32).astype(BF16)
    place = (zi - zo) * 3 + (yi - yo + 1)
    valid = (yi - yo + 1 >= 0) & (yi - yo + 1 <= 2) & (zi - zo >= 0) & (zi - zo <= 2)
    place = jnp.where(valid, place, -1)
    keeps = {
        "all": None,
        "middle": ((zi >= 2) == (zo == 1)) | inner,
        "low": (zi <= 2) | inner,
        "high": (zi >= 1) | inner,
    }
    wide = dot(conv, spread_cols).astype(BF16)
    for e in range(3):
        total = jnp.zeros((128, 256), F32)
        for ab in range(9):
            at = (ab * 3 + e) * CH
            total = jnp.where(place == ab, dot(spread_rows, wide[at : at + CH]), total)
        total = total * 0.5
        for out, name in outs:
            part = total if keeps[name] is None else jnp.where(keeps[name], total, 0.0)
            out[:, e * 256 : (e + 1) * 256] = part.astype(BF16)


def silu_of_half(h):
    return h + h * jnp.tanh(h)


def across(column, width):
    return jnp.concatenate([column] * (width // INNER), axis=1)


def shifts(ref, row, value):
    lane = lax.broadcasted_iota(jnp.int32, (16, NX), 1)
    none = jnp.zeros_like(value)
    ref[0, row : row + 16, :] = jnp.where(lane == 0, none, pltpu.roll(value, 1, 1))
    ref[2, row : row + 16, :] = jnp.where(lane == NX - 1, none, pltpu.roll(value, NX - 1, 1))


def lift(slab_ref, x_ref, par_ref):
    for z in range(DEPTH):
        cells = jnp.concatenate([slab_ref[z]] * 4, axis=0)
        for block in range(4):
            rows = slice(block * 16, block * 16 + 16)
            value = silu_of_half(across(par_ref[0, rows], NX) * cells + across(par_ref[1, rows], NX))
            value = value.astype(BF16)
            x_ref[1, z * 64 + block * 16 : z * 64 + block * 16 + 16, :] = value
            shifts(x_ref, z * 64 + block * 16, value)


def shift_rows(x_ref, first, count):
    for block in range(count):
        row = first + block * 16
        shifts(x_ref, row, x_ref[1, row : row + 16, :])


CHUNK = 256


def convolve(w_ref, parts, bias, at):
    total = bias
    for e in range(3):
        cells = [ref[e, row : row + size, at : at + CHUNK] for ref, row, size in parts]
        cells = cells[0] if len(cells) == 1 else jnp.concatenate(cells, 0)
        total = total + dot(w_ref[:, e * 256 : (e + 1) * 256], cells)
    return silu_of_half(total)


def bias_of(par_ref, index):
    return across(jnp.concatenate([par_ref[index]] * 2, 0), CHUNK)


def prepare_kernel(
    at_ref, slab_ref, small_ref, par_ref, w1_ref, w1m_ref, w2a_ref, w2b_ref, x1_ref, x2_ref
):
    channel = lax.broadcasted_iota(jnp.int32, (4 * CH, CH), 0) // 4
    mine = channel == lax.broadcasted_iota(jnp.int32, (4 * CH, CH), 1)
    for index in range(5):
        values = small_ref[2 * 27 * CH + index : 2 * 27 * CH + index + 1, :]
        column = jnp.sum(jnp.where(mine, values, 0.0), axis=1, keepdims=True)
        if index < 4:
            column = 0.5 * column
        par_ref[index] = jnp.broadcast_to(column, (4 * CH, INNER))
    first = small_ref[: 27 * CH].astype(BF16)
    second = small_ref[27 * CH : 2 * 27 * CH].astype(BF16)
    inner = at_ref[0] > 0
    build_weights(inner, first, ((w1_ref, "all"), (w1m_ref, "middle")))
    build_weights(inner, second, ((w2a_ref, "low"), (w2b_ref, "high")))
    lift(slab_ref, x1_ref, par_ref)
    bias = bias_of(par_ref, 2)
    for at in range(0, NX, CHUNK):
        act = convolve(w1_ref, ((x1_ref, 0, 256),), bias, at)
        x2_ref[1, :, at : at + CHUNK] = act.astype(BF16)
    shift_rows(x2_ref, 0, 8)


def filter_kernel(
    left_ref, own_ref, par_ref, w1_ref, w1m_ref, w2a_ref, w2b_ref, x1_ref, x2_ref,
    full_ref, ends_ref, twiddle_ref, out_ref, x1, x2,
):
    lift(left_ref, x1, par_ref)
    bias = bias_of(par_ref, 2)
    for at in range(0, NX, CHUNK):
        act = convolve(w1_ref, ((x1, 0, 256),), bias, at)
        x2[1, :128, at : at + CHUNK] = act.astype(BF16)
        act = convolve(w1m_ref, ((x1, 128, 128), (x1_ref, 0, 128)), bias, at)
        x2[1, 128:, at : at + CHUNK] = act.astype(BF16)
    shift_rows(x2, 0, 16)
    bias = bias_of(par_ref, 3)
    mix = across(par_ref[4], CHUNK)
    a = []
    for at in range(0, NX, CHUNK):
        slices = []
        for w_ref, parts in (
            (w2a_ref, ((x2, 0, 256),)),
            (w2b_ref, ((x2, 128, 128), (x2_ref, 0, 128))),
        ):
            act = convolve(w_ref, parts, bias, at)
            for zo in range(2):
                terms = act[zo * 64 : zo * 64 + 64] * mix
                total = terms[0:8]
                for pair in range(1, 8):
                    total = total + terms[pair * 8 : pair * 8 + 8]
                z = 2 + len(slices)
                base = left_ref[z, :, at : at + CHUNK] if z < DEPTH else own_ref[z - DEPTH, :, at : at + CHUNK]
                slices.append(base + total[0:4] + total[4:8])
        mixed = jnp.concatenate([slices[z][y : y + 1] for y in range(NY) for z in range(DEPTH)], 0)
        a += [mixed[:, i : i + INNER] for i in range(0, CHUNK, INNER)]
    forward(a, full_ref, ends_ref, twiddle_ref, out_ref)


def cos16(n):
    return math.cos(2 * math.pi * (n % 16) / 16)


def sin16(n):
    return math.sin(2 * math.pi * (n % 16) / 16)


def weigh(terms):
    total = None
    for factor, value in terms:
        if abs(factor) < 1e-9:
            continue
        if abs(factor - 1) < 1e-9:
            term = value
        elif abs(factor + 1) < 1e-9:
            term = -value
        else:
            term = value * factor
        total = term if total is None else total + term
    return total


def forward(a, full_ref, ends_ref, twiddle_ref, out_ref):
    plus = [a[i] + a[16 - i] for i in range(1, 8)]
    minus = [a[i] - a[16 - i] for i in range(1, 8)]
    re, im = [], []
    for k1 in range(9):
        re.append(weigh([(1, a[0]), ((-1) ** k1, a[8])] + [(cos16(k1 * i), plus[i - 1]) for i in range(1, 8)]))
        im.append(weigh([(-sin16(k1 * i), minus[i - 1]) for i in range(1, 8)]))
    rows = []
    for k1 in range(1, 8):
        c, s = twiddle_ref[k1 - 1 : k1], twiddle_ref[k1 + 7 : k1 + 8]
        rows.append(jnp.concatenate([re[k1] * c + im[k1] * s, im[k1] * c - re[k1] * s], 1))
    whole = dot(jnp.concatenate(rows, 0).astype(BF16), full_ref[...])
    blocks = [
        dot(re[0].astype(BF16), ends_ref[:, :INNER]),
        dot(re[8].astype(BF16), ends_ref[:, INNER:]),
    ]
    for k1 in range(1, 8):
        for h in range(2):
            blocks.append(whole[(k1 - 1) * 16 : k1 * 16, h * INNER : (h + 1) * INNER])
    for y in range(NY):
        for b in range(BLOCKS):
            out_ref[y * BLOCKS + b] = blocks[b][y * DEPTH : (y + 1) * DEPTH].astype(BF16)


def inverse_kernel(in_ref, full_ref, ends_ref, twiddle_ref, out_ref):
    blocks = [
        jnp.concatenate([in_ref[y * BLOCKS + b].astype(F32) for y in range(NY)], 0).astype(BF16)
        for b in range(BLOCKS)
    ]
    even = dot(blocks[0], ends_ref[:, :INNER])
    mid = dot(blocks[1], ends_ref[:, INNER:])
    lows = jnp.concatenate([blocks[2 * k1] for k1 in range(1, 8)], 0)
    highs = jnp.concatenate([blocks[2 * k1 + 1] for k1 in range(1, 8)], 0)
    whole = dot(lows, full_ref[:INNER]) + dot(highs, full_ref[INNER:])
    re, im = [], []
    for k1 in range(1, 8):
        part = whole[(k1 - 1) * 16 : k1 * 16]
        b_re, b_im = part[:, :INNER], part[:, INNER:]
        c, s = twiddle_ref[k1 - 1 : k1], twiddle_ref[k1 + 7 : k1 + 8]
        re.append(b_re * c - b_im * s)
        im.append(b_re * s + b_im * c)
    scale = 1.0 / (NX * NZ)
    even, mid = even * scale, mid * scale
    re, im = [v * scale for v in re], [v * scale for v in im]
    out = [None] * RADIX
    for x1 in range(9):
        p = weigh([(1, even), ((-1) ** x1, mid)] + [(cos16(k1 * x1), re[k1 - 1]) for k1 in range(1, 8)])
        q = weigh([(sin16(k1 * x1), im[k1 - 1]) for k1 in range(1, 8)])
        if q is None:
            out[x1] = p
        else:
            out[x1], out[16 - x1] = p - q, p + q
    for x1 in range(RADIX):
        for z in range(DEPTH):
            rows = [out[x1][y * DEPTH + z : y * DEPTH + z + 1] for y in range(NY)]
            out_ref[z, :, x1 * INNER : (x1 + 1) * INNER] = jnp.concatenate(rows, 0)


def wedge_kernel(at_ref, wedge_ref, plus_ref, minus_ref):
    block = at_ref[0] % BLOCKS
    k = lax.broadcasted_iota(jnp.int32, (NX, INNER), 0)
    j = lax.broadcasted_iota(jnp.int32, (NX, INNER), 1)
    col = j % HALF
    k1 = jnp.where(block == 0, 0, jnp.where(block == 1, 8, block // 2))
    high = jnp.where(block < 2, 0, block % 2)
    mine = k1 + RADIX * (HALF * high + col)
    target = jnp.where(j < HALF, mine, (NX - mine) % NX)
    special = (block == 0) & (col == 0)
    quarter = special & (k == NX // 2)
    hit = (k == target)
    plain = jnp.where(hit, jnp.where(special, 0.25, 1.0), 0.0) + jnp.where(quarter, 0.25, 0.0)
    cross = jnp.where(special, jnp.where(hit, 0.25, 0.0) - jnp.where(quarter, 0.25, 0.0), 0.0)
    select = jnp.concatenate([plain, cross], 1).astype(BF16)
    whole = wedge_ref[...]
    top = whole.astype(BF16)
    rest = (whole - top.astype(F32)).astype(BF16)
    picked = dot(top, select) + dot(rest, select)
    r = lax.broadcasted_iota(jnp.int32, (NZ, NZ), 0)
    c = lax.broadcasted_iota(jnp.int32, (NZ, NZ), 1)
    flip = ((r + c) % NZ == 0).astype(F32).astype(BF16)
    top = picked.astype(BF16)
    rest = (picked - top.astype(F32)).astype(BF16)
    turned = dot(flip, top) + dot(flip, rest)
    low = lax.broadcasted_iota(jnp.int32, (NZ, INNER), 1) < HALF
    for out, at in ((plus_ref, 0), (minus_ref, INNER)):
        here, there = picked[:, at : at + INNER], turned[:, at : at + INNER]
        both = jnp.where(low, here + pltpu.roll(there, HALF, 1), there + pltpu.roll(here, HALF, 1))
        out[...] = both


def middle_kernel(own_ref, other_ref, plus_ref, minus_ref, ahead_ref, back_ref, out_ref):
    delta = (own_ref[...].astype(F32) - other_ref[...].astype(F32)).astype(BF16)
    sign = jnp.where(lax.broadcasted_iota(jnp.int32, (NZ, INNER), 1) < HALF, 1.0, -1.0)
    both = dot(ahead_ref[...], delta)
    cos_part, sin_part = both[:NZ], pltpu.roll(both[NZ:], HALF, 1)
    freq = cos_part + sign * sin_part
    mirror = sign * cos_part - sin_part
    weighted = (plus_ref[...] * freq + minus_ref[...] * mirror).astype(BF16)
    both = dot(back_ref[...], weighted)
    out_ref[...] = (both[:NZ] - sign * pltpu.roll(both[NZ:], HALF, 1)).astype(BF16)


def call(kernel, outs, *args, scratch=(), megabytes=8, smem=0, flops=10**7):
    many = isinstance(outs, list)
    spec = lambda space: pl.BlockSpec(memory_space=space)
    moved = sum(a.size * a.dtype.itemsize for a in args)
    return pl.pallas_call(
        kernel,
        out_shape=outs,
        in_specs=[spec(pltpu.SMEM)] * smem + [spec(pltpu.VMEM)] * (len(args) - smem),
        out_specs=[spec(pltpu.VMEM)] * len(outs) if many else spec(pltpu.VMEM),
        scratch_shapes=scratch,
        compiler_params=params(megabytes),
        cost_estimate=pl.CostEstimate(flops=flops, bytes_accessed=moved, transcendentals=0),
    )(*args)


def shape(*dims, dtype=BF16):
    return jax.ShapeDtypeStruct(dims, dtype)


def body(
    density,
    lift_weight,
    lift_bias,
    conv_first,
    bias_first,
    conv_second,
    bias_second,
    projection,
    wedge,
):
    full_x, ends_x, full_i, ends_i, twiddle = x_tables()
    ahead, back = z_tables()
    place = lax.axis_index("gz")
    slab = density[0]
    left = lax.ppermute(slab, "gz", [(i, (i + 1) % GZ) for i in range(GZ)])

    flat = lambda w: w.transpose(2, 3, 4, 0, 1).reshape(27 * CH, CH)
    at = place.astype(jnp.int32).reshape(1)
    vectors = jnp.stack([lift_weight, lift_bias, bias_first, bias_second, projection])
    small = jnp.concatenate([flat(conv_first).astype(F32), flat(conv_second).astype(F32), vectors], 0)
    par, w1, w1m, w2a, w2b, x1, x2 = call(
        prepare_kernel,
        [shape(5, 4 * CH, INNER, dtype=F32)] + [shape(128, 768)] * 4 + [shape(3, 256, NX), shape(3, 128, NX)],
        at, slab, small, smem=1, megabytes=24, flops=10**9,
    )
    plus, minus = call(
        wedge_kernel, [shape(NZ, INNER, dtype=F32)] * 2, at, wedge, smem=1, megabytes=16, flops=10**9,
    )
    spectrum = call(
        filter_kernel, shape(GZ, DEPTH, INNER), left, slab, par, w1, w1m, w2a, w2b, x1, x2,
        full_x, ends_x, twiddle,
        scratch=[pltpu.VMEM((3, 256, NX), BF16), pltpu.VMEM((3, 256, NX), BF16)],
        megabytes=24, flops=10**9,
    )
    pencils = lax.all_to_all(spectrum, "gz", split_axis=0, concat_axis=0, tiled=True)
    pencils = pencils.reshape(NZ, INNER)
    other = lax.ppermute(pencils, "half", [(i, i ^ 1) for i in range(lax.axis_size("half"))])
    returned = call(
        middle_kernel, shape(NZ, INNER), pencils, other, plus, minus, ahead, back,
    )
    slabs = lax.all_to_all(
        returned.reshape(GZ, DEPTH, INNER), "gz", split_axis=0, concat_axis=0, tiled=True
    )
    residual = call(
        inverse_kernel, shape(DEPTH, NY, NX, dtype=F32), slabs, full_i, ends_i, twiddle,
    )
    return residual[None]


def solution(mesh):
    placed = (P("half", "gz", None, None), P(), P(), P(), P(), P(), P(), P(), P())
    return jax.shard_map(
        body, mesh=mesh, in_specs=placed, out_specs=P("half", "gz", None, None), check_vma=False
    )
```

```python
import math

import jax
import jax.numpy as jnp
import numpy as np
from jax import lax
from jax.experimental import pallas as pl
from jax.experimental.pallas import tpu as pltpu
from jax.sharding import PartitionSpec as P

NX, CH, NY, NZ = 2048, 16, 4, 256
GZ = 64
DEPTH = NZ // GZ
RADIX, INNER = 16, NX // 16
HALF = INNER // 2
BLOCKS = 16
LAG = 2
F32, BF16 = jnp.float32, jnp.bfloat16


def dot(a, b):
    return jnp.dot(a, b, preferred_element_type=F32)


def params(megabytes=8):
    return pltpu.CompilerParams(vmem_limit_bytes=megabytes << 20)


def turn(product, size):
    angle = 2.0 * math.pi * (product % size) / size
    return np.cos(angle), np.sin(angle)


def x_tables():
    x0 = np.arange(INNER)[:, None]
    k0 = np.arange(INNER)[None, :]
    c, s = turn(x0 * k0, INNER)
    pick = lambda t, h: t[:, h * HALF : (h + 1) * HALF]
    from_re = np.concatenate([pick(c, 0), pick(-s, 0), pick(c, 1), pick(-s, 1)], 1)
    from_im = np.concatenate([pick(s, 0), pick(c, 0), pick(s, 1), pick(c, 1)], 1)
    full = np.concatenate([from_re, from_im], 0)
    first = np.concatenate([pick(c, 0), pick(-s, 0)], 1)
    first[:, HALF] = c[:, HALF]
    c8, s8 = turn(x0 * (1 + 2 * np.arange(HALF)[None, :]), 2 * INNER)
    middle = np.concatenate([c8, -s8], 1)
    k1 = np.arange(1, 8)[:, None]
    ct, st = turn(k1 * np.arange(INNER)[None, :], NX)
    twiddle = np.concatenate([ct, np.zeros((1, INNER)), st, np.zeros((1, INNER))], 0)
    return (
        full.astype(jnp.bfloat16),
        np.concatenate([first, middle], 1).astype(jnp.bfloat16),
        full.T.astype(jnp.bfloat16),
        np.concatenate([first.T, middle.T], 1).astype(jnp.bfloat16),
        twiddle.astype(np.float32),
    )


def z_tables():
    kz = np.arange(NZ)[:, None]
    row = np.arange(NZ)[None, :]
    ahead = np.concatenate(turn(kz * (row - LAG), NZ), 0)
    back = np.concatenate(turn(kz * row, NZ), 0)
    return ahead.astype(jnp.bfloat16), back.astype(jnp.bfloat16)


def build_weights(inner, conv_ref, layer, outs):
    rows = lax.broadcasted_iota(jnp.int32, (128, 256), 0)
    cols = lax.broadcasted_iota(jnp.int32, (128, 256), 1)
    zo, yo = rows // 64, rows % 4
    zi, yi = cols // 64, cols % 4
    spread_rows = (
        lax.broadcasted_iota(jnp.int32, (128, CH), 0) % 64 // 4
        == lax.broadcasted_iota(jnp.int32, (128, CH), 1)
    ).astype(F32).astype(BF16)
    spread_cols = (
        lax.broadcasted_iota(jnp.int32, (CH, 256), 1) % 64 // 4
        == lax.broadcasted_iota(jnp.int32, (CH, 256), 0)
    ).astype(F32).astype(BF16)
    place = (zi - zo) * 3 + (yi - yo + 1)
    valid = (yi - yo + 1 >= 0) & (yi - yo + 1 <= 2) & (zi - zo >= 0) & (zi - zo <= 2)
    place = jnp.where(valid, place, -1)
    keeps = {
        "all": None,
        "middle": ((zi >= 2) == (zo == 1)) | inner,
        "low": (zi <= 2) | inner,
        "high": (zi >= 1) | inner,
    }
    wide = dot(conv_ref[...], spread_cols).astype(BF16)
    for e in range(3):
        total = jnp.zeros((128, 256), F32)
        for ab in range(9):
            at = ((ab * 3 + e) * 2 + layer) * CH
            total = jnp.where(place == ab, dot(spread_rows, wide[at : at + CH]), total)
        total = total * 0.5
        for out, name in outs:
            part = total if keeps[name] is None else jnp.where(keeps[name], total, 0.0)
            out[:, e * 256 : (e + 1) * 256] = part.astype(BF16)


def silu_of_half(h):
    return h + h * jnp.tanh(h)


def across(column, width):
    return jnp.concatenate([column] * (width // INNER), axis=1)


def shifts(ref, row, value):
    lane = lax.broadcasted_iota(jnp.int32, (16, NX), 1)
    none = jnp.zeros_like(value)
    ref[0, row : row + 16, :] = jnp.where(lane == 0, none, pltpu.roll(value, 1, 1))
    ref[2, row : row + 16, :] = jnp.where(lane == NX - 1, none, pltpu.roll(value, NX - 1, 1))


def lift(slab_ref, x_ref, par_ref):
    for z in range(DEPTH):
        cells = jnp.concatenate([slab_ref[z].astype(F32)] * 4, axis=0)
        for block in range(4):
            rows = slice(block * 16, block * 16 + 16)
            value = silu_of_half(across(par_ref[0, rows], NX) * cells + across(par_ref[1, rows], NX))
            value = value.astype(BF16)
            x_ref[1, z * 64 + block * 16 : z * 64 + block * 16 + 16, :] = value
            shifts(x_ref, z * 64 + block * 16, value)


def shift_rows(x_ref, first, count):
    for block in range(count):
        row = first + block * 16
        shifts(x_ref, row, x_ref[1, row : row + 16, :])


CHUNK = 256


def convolve(w_ref, parts, bias, at):
    total = bias
    for e in range(3):
        cells = [ref[e, row : row + size, at : at + CHUNK] for ref, row, size in parts]
        cells = cells[0] if len(cells) == 1 else jnp.concatenate(cells, 0)
        total = total + dot(w_ref[:, e * 256 : (e + 1) * 256], cells)
    return silu_of_half(total)


def bias_of(par_ref, index):
    return across(jnp.concatenate([par_ref[index]] * 2, 0), CHUNK)


def prepare_kernel(
    at_ref, slab_ref, conv_ref, vector_ref, par_ref, w1_ref, w1m_ref, w2a_ref, w2b_ref, x1_ref, x2_ref
):
    channel = lax.broadcasted_iota(jnp.int32, (4 * CH, CH), 0) // 4
    mine = channel == lax.broadcasted_iota(jnp.int32, (4 * CH, CH), 1)
    for index in range(5):
        values = vector_ref[index : index + 1, :]
        column = jnp.sum(jnp.where(mine, values, 0.0), axis=1, keepdims=True)
        if index < 4:
            column = 0.5 * column
        par_ref[index] = jnp.broadcast_to(column, (4 * CH, INNER))
    inner = at_ref[0] > 0
    build_weights(inner, conv_ref, 0, ((w1_ref, "all"), (w1m_ref, "middle")))
    build_weights(inner, conv_ref, 1, ((w2a_ref, "low"), (w2b_ref, "high")))
    lift(slab_ref, x1_ref, par_ref)
    bias = bias_of(par_ref, 2)
    for at in range(0, NX, CHUNK):
        act = convolve(w1_ref, ((x1_ref, 0, 256),), bias, at)
        x2_ref[1, :, at : at + CHUNK] = act.astype(BF16)
    shift_rows(x2_ref, 0, 8)


def filter_kernel(
    left_ref, own_ref, par_ref, w1_ref, w1m_ref, w2a_ref, w2b_ref, x1_ref, x2_ref,
    full_ref, ends_ref, twiddle_ref, out_ref, x1, x2,
):
    lift(left_ref, x1, par_ref)
    bias = bias_of(par_ref, 2)
    for at in range(0, NX, CHUNK):
        act = convolve(w1_ref, ((x1, 0, 256),), bias, at)
        x2[1, :128, at : at + CHUNK] = act.astype(BF16)
        act = convolve(w1m_ref, ((x1, 128, 128), (x1_ref, 0, 128)), bias, at)
        x2[1, 128:, at : at + CHUNK] = act.astype(BF16)
    shift_rows(x2, 0, 16)
    bias = bias_of(par_ref, 3)
    mix = across(par_ref[4], CHUNK)
    a = []
    for at in range(0, NX, CHUNK):
        slices = []
        for w_ref, parts in (
            (w2a_ref, ((x2, 0, 256),)),
            (w2b_ref, ((x2, 128, 128), (x2_ref, 0, 128))),
        ):
            act = convolve(w_ref, parts, bias, at)
            for zo in range(2):
                terms = act[zo * 64 : zo * 64 + 64] * mix
                total = terms[0:8]
                for pair in range(1, 8):
                    total = total + terms[pair * 8 : pair * 8 + 8]
                z = 2 + len(slices)
                cells_ref = left_ref if z < DEPTH else own_ref
                base = cells_ref[z % DEPTH, :, at : at + CHUNK].astype(F32)
                slices.append(base + total[0:4] + total[4:8])
        mixed = jnp.concatenate([slices[z][y : y + 1] for y in range(NY) for z in range(DEPTH)], 0)
        a += [mixed[:, i : i + INNER] for i in range(0, CHUNK, INNER)]
    forward(a, full_ref, ends_ref, twiddle_ref, out_ref)


def cos16(n):
    return math.cos(2 * math.pi * (n % 16) / 16)


def sin16(n):
    return math.sin(2 * math.pi * (n % 16) / 16)


def weigh(terms):
    total = None
    for factor, value in terms:
        if abs(factor) < 1e-9:
            continue
        if abs(factor - 1) < 1e-9:
            term = value
        elif abs(factor + 1) < 1e-9:
            term = -value
        else:
            term = value * factor
        total = term if total is None else total + term
    return total


def forward(a, full_ref, ends_ref, twiddle_ref, out_ref):
    plus = [a[i] + a[16 - i] for i in range(1, 8)]
    minus = [a[i] - a[16 - i] for i in range(1, 8)]
    re, im = [], []
    for k1 in range(9):
        re.append(weigh([(1, a[0]), ((-1) ** k1, a[8])] + [(cos16(k1 * i), plus[i - 1]) for i in range(1, 8)]))
        im.append(weigh([(-sin16(k1 * i), minus[i - 1]) for i in range(1, 8)]))
    rows = []
    for k1 in range(1, 8):
        c, s = twiddle_ref[k1 - 1 : k1], twiddle_ref[k1 + 7 : k1 + 8]
        rows.append(jnp.concatenate([re[k1] * c + im[k1] * s, im[k1] * c - re[k1] * s], 1))
    whole = dot(jnp.concatenate(rows, 0).astype(BF16), full_ref[...])
    blocks = [
        dot(re[0].astype(BF16), ends_ref[:, :INNER]),
        dot(re[8].astype(BF16), ends_ref[:, INNER:]),
    ]
    for k1 in range(1, 8):
        for h in range(2):
            blocks.append(whole[(k1 - 1) * 16 : k1 * 16, h * INNER : (h + 1) * INNER])
    for y in range(NY):
        for b in range(BLOCKS):
            out_ref[y * BLOCKS + b] = blocks[b][y * DEPTH : (y + 1) * DEPTH].astype(BF16)


def inverse_kernel(in_ref, full_ref, ends_ref, twiddle_ref, out_ref):
    blocks = [
        jnp.concatenate([in_ref[y * BLOCKS + b].astype(F32) for y in range(NY)], 0).astype(BF16)
        for b in range(BLOCKS)
    ]
    even = dot(blocks[0], ends_ref[:, :INNER])
    mid = dot(blocks[1], ends_ref[:, INNER:])
    lows = jnp.concatenate([blocks[2 * k1] for k1 in range(1, 8)], 0)
    highs = jnp.concatenate([blocks[2 * k1 + 1] for k1 in range(1, 8)], 0)
    whole = dot(lows, full_ref[:INNER]) + dot(highs, full_ref[INNER:])
    re, im = [], []
    for k1 in range(1, 8):
        part = whole[(k1 - 1) * 16 : k1 * 16]
        b_re, b_im = part[:, :INNER], part[:, INNER:]
        c, s = twiddle_ref[k1 - 1 : k1], twiddle_ref[k1 + 7 : k1 + 8]
        re.append(b_re * c - b_im * s)
        im.append(b_re * s + b_im * c)
    scale = 1.0 / (NX * NZ)
    even, mid = even * scale, mid * scale
    re, im = [v * scale for v in re], [v * scale for v in im]
    out = [None] * RADIX
    for x1 in range(9):
        p = weigh([(1, even), ((-1) ** x1, mid)] + [(cos16(k1 * x1), re[k1 - 1]) for k1 in range(1, 8)])
        q = weigh([(sin16(k1 * x1), im[k1 - 1]) for k1 in range(1, 8)])
        if q is None:
            out[x1] = p
        else:
            out[x1], out[16 - x1] = p - q, p + q
    for x1 in range(RADIX):
        for z in range(DEPTH):
            rows = [out[x1][y * DEPTH + z : y * DEPTH + z + 1] for y in range(NY)]
            out_ref[z, :, x1 * INNER : (x1 + 1) * INNER] = jnp.concatenate(rows, 0)


def wedge_kernel(at_ref, wedge_ref, plus_ref, minus_ref):
    block = at_ref[0] % BLOCKS
    k = lax.broadcasted_iota(jnp.int32, (NX, INNER), 0)
    j = lax.broadcasted_iota(jnp.int32, (NX, INNER), 1)
    col = j % HALF
    k1 = jnp.where(block == 0, 0, jnp.where(block == 1, 8, block // 2))
    high = jnp.where(block < 2, 0, block % 2)
    mine = k1 + RADIX * (HALF * high + col)
    target = jnp.where(j < HALF, mine, (NX - mine) % NX)
    special = (block == 0) & (col == 0)
    quarter = special & (k == NX // 2)
    hit = (k == target)
    plain = jnp.where(hit, jnp.where(special, 0.25, 1.0), 0.0) + jnp.where(quarter, 0.25, 0.0)
    cross = jnp.where(special, jnp.where(hit, 0.25, 0.0) - jnp.where(quarter, 0.25, 0.0), 0.0)
    select = jnp.concatenate([plain, cross], 1).astype(BF16)
    whole = wedge_ref[...]
    top = whole.astype(BF16)
    rest = (whole - top.astype(F32)).astype(BF16)
    picked = dot(top, select) + dot(rest, select)
    r = lax.broadcasted_iota(jnp.int32, (NZ, NZ), 0)
    c = lax.broadcasted_iota(jnp.int32, (NZ, NZ), 1)
    flip = ((r + c) % NZ == 0).astype(F32).astype(BF16)
    top = picked.astype(BF16)
    rest = (picked - top.astype(F32)).astype(BF16)
    turned = dot(flip, top) + dot(flip, rest)
    low = lax.broadcasted_iota(jnp.int32, (NZ, INNER), 1) < HALF
    for out, at in ((plus_ref, 0), (minus_ref, INNER)):
        here, there = picked[:, at : at + INNER], turned[:, at : at + INNER]
        both = jnp.where(low, here + pltpu.roll(there, HALF, 1), there + pltpu.roll(here, HALF, 1))
        out[...] = both


def middle_kernel(own_ref, other_ref, plus_ref, minus_ref, ahead_ref, back_ref, out_ref):
    delta = (own_ref[...].astype(F32) - other_ref[...].astype(F32)).astype(BF16)
    sign = jnp.where(lax.broadcasted_iota(jnp.int32, (NZ, INNER), 1) < HALF, 1.0, -1.0)
    both = dot(ahead_ref[...], delta)
    cos_part, sin_part = both[:NZ], pltpu.roll(both[NZ:], HALF, 1)
    freq = cos_part + sign * sin_part
    mirror = sign * cos_part - sin_part
    weighted = (plus_ref[...] * freq + minus_ref[...] * mirror).astype(BF16)
    both = dot(back_ref[...], weighted)
    out_ref[...] = (both[:NZ] - sign * pltpu.roll(both[NZ:], HALF, 1)).astype(BF16)


def call(kernel, outs, *args, scratch=(), megabytes=8, smem=0, flops=10**7):
    many = isinstance(outs, list)
    spec = lambda space: pl.BlockSpec(memory_space=space)
    moved = sum(a.size * a.dtype.itemsize for a in args)
    return pl.pallas_call(
        kernel,
        out_shape=outs,
        in_specs=[spec(pltpu.SMEM)] * smem + [spec(pltpu.VMEM)] * (len(args) - smem),
        out_specs=[spec(pltpu.VMEM)] * len(outs) if many else spec(pltpu.VMEM),
        scratch_shapes=scratch,
        compiler_params=params(megabytes),
        cost_estimate=pl.CostEstimate(flops=flops, bytes_accessed=moved, transcendentals=0),
    )(*args)


def shape(*dims, dtype=BF16):
    return jax.ShapeDtypeStruct(dims, dtype)


def body(
    density,
    lift_weight,
    lift_bias,
    conv_first,
    bias_first,
    conv_second,
    bias_second,
    projection,
    wedge,
):
    full_x, ends_x, full_i, ends_i, twiddle = x_tables()
    ahead, back = z_tables()
    place = lax.axis_index("gz")
    slab = density[0]
    rounded = slab.astype(BF16)
    left = lax.ppermute(rounded, "gz", [(i, (i + 1) % GZ) for i in range(GZ)])

    at = place.astype(jnp.int32).reshape(1)
    vectors = jnp.stack([lift_weight, lift_bias, bias_first, bias_second, projection])
    convs = jnp.concatenate([conv_first, conv_second], 0).transpose(2, 3, 4, 0, 1).reshape(54 * CH, CH)
    par, w1, w1m, w2a, w2b, x1, x2 = call(
        prepare_kernel,
        [shape(5, 4 * CH, INNER, dtype=F32)] + [shape(128, 768)] * 4 + [shape(3, 256, NX), shape(3, 128, NX)],
        at, rounded, convs, vectors, smem=1, megabytes=24, flops=10**9,
    )
    plus, minus = call(
        wedge_kernel, [shape(NZ, INNER, dtype=F32)] * 2, at, wedge, smem=1, megabytes=16, flops=10**9,
    )
    spectrum = call(
        filter_kernel, shape(GZ, DEPTH, INNER), left, slab, par, w1, w1m, w2a, w2b, x1, x2,
        full_x, ends_x, twiddle,
        scratch=[pltpu.VMEM((3, 256, NX), BF16), pltpu.VMEM((3, 256, NX), BF16)],
        megabytes=24, flops=10**9,
    )
    pencils = lax.all_to_all(spectrum, "gz", split_axis=0, concat_axis=0, tiled=True)
    pencils = pencils.reshape(NZ, INNER)
    other = lax.ppermute(pencils, "half", [(i, i ^ 1) for i in range(lax.axis_size("half"))])
    returned = call(
        middle_kernel, shape(NZ, INNER), pencils, other, plus, minus, ahead, back,
    )
    slabs = lax.all_to_all(
        returned.reshape(GZ, DEPTH, INNER), "gz", split_axis=0, concat_axis=0, tiled=True
    )
    residual = call(
        inverse_kernel, shape(DEPTH, NY, NX, dtype=F32), slabs, full_i, ends_i, twiddle,
    )
    return residual[None]


def solution(mesh):
    placed = (P("half", "gz", None, None), P(), P(), P(), P(), P(), P(), P(), P())
    return jax.shard_map(
        body, mesh=mesh, in_specs=placed, out_specs=P("half", "gz", None, None), check_vma=False
    )
```

```python
import math

import jax
import jax.numpy as jnp
import numpy as np
from jax import lax
from jax.experimental import pallas as pl
from jax.experimental.pallas import tpu as pltpu
from jax.sharding import PartitionSpec as P

NX, CH, NY, NZ = 2048, 16, 4, 256
GZ = 64
DEPTH = NZ // GZ
RADIX, INNER = 16, NX // 16
HALF = INNER // 2
BLOCKS = 16
LAG = 2
F32, BF16 = jnp.float32, jnp.bfloat16
ORDER = (
    46, 24, 10, 23, 29, 15, 43, 25, 3, 9, 1, 17, 8, 58, 26, 4,
    50, 42, 41, 38, 62, 14, 33, 5, 21, 31, 28, 57, 44, 18, 51, 34,
    45, 61, 54, 22, 35, 11, 20, 39, 32, 12, 47, 7, 37, 6, 27, 36,
    56, 52, 16, 63, 2, 30, 40, 19, 55, 13, 0, 60, 53, 59, 49, 48,
)
RANK = tuple(ORDER.index(i) for i in range(GZ))


def dot(a, b):
    return jnp.dot(a, b, preferred_element_type=F32)


def params(megabytes=8):
    return pltpu.CompilerParams(vmem_limit_bytes=megabytes << 20)


def turn(product, size):
    angle = 2.0 * math.pi * (product % size) / size
    return np.cos(angle), np.sin(angle)


def x_tables():
    x0 = np.arange(INNER)[:, None]
    k0 = np.arange(INNER)[None, :]
    c, s = turn(x0 * k0, INNER)
    pick = lambda t, h: t[:, h * HALF : (h + 1) * HALF]
    from_re = np.concatenate([pick(c, 0), pick(-s, 0), pick(c, 1), pick(-s, 1)], 1)
    from_im = np.concatenate([pick(s, 0), pick(c, 0), pick(s, 1), pick(c, 1)], 1)
    full = np.concatenate([from_re, from_im], 0)
    first = np.concatenate([pick(c, 0), pick(-s, 0)], 1)
    first[:, HALF] = c[:, HALF]
    c8, s8 = turn(x0 * (1 + 2 * np.arange(HALF)[None, :]), 2 * INNER)
    middle = np.concatenate([c8, -s8], 1)
    k1 = np.arange(1, 8)[:, None]
    ct, st = turn(k1 * np.arange(INNER)[None, :], NX)
    twiddle = np.concatenate([ct, np.zeros((1, INNER)), st, np.zeros((1, INNER))], 0)
    return (
        full.astype(jnp.bfloat16),
        np.concatenate([first, middle], 1).astype(jnp.bfloat16),
        full.T.astype(jnp.bfloat16),
        np.concatenate([first.T, middle.T], 1).astype(jnp.bfloat16),
        twiddle.astype(np.float32),
    )


def z_tables():
    kz = np.arange(NZ)
    z = (DEPTH * np.array(ORDER)[:, None] + np.arange(DEPTH)[None, :]).reshape(NZ)
    ahead = np.concatenate(turn(kz[:, None] * (z - LAG)[None, :], NZ), 0)
    back = np.concatenate(turn(z[:, None] * kz[None, :], NZ), 0)
    return ahead.astype(jnp.bfloat16), back.astype(jnp.bfloat16)


def build_weights(inner, conv_ref, layer, outs):
    rows = lax.broadcasted_iota(jnp.int32, (128, 256), 0)
    cols = lax.broadcasted_iota(jnp.int32, (128, 256), 1)
    zo, yo = rows // 64, rows % 4
    zi, yi = cols // 64, cols % 4
    spread_rows = (
        lax.broadcasted_iota(jnp.int32, (128, CH), 0) % 64 // 4
        == lax.broadcasted_iota(jnp.int32, (128, CH), 1)
    ).astype(F32).astype(BF16)
    spread_cols = (
        lax.broadcasted_iota(jnp.int32, (CH, 256), 1) % 64 // 4
        == lax.broadcasted_iota(jnp.int32, (CH, 256), 0)
    ).astype(F32).astype(BF16)
    place = (zi - zo) * 3 + (yi - yo + 1)
    valid = (yi - yo + 1 >= 0) & (yi - yo + 1 <= 2) & (zi - zo >= 0) & (zi - zo <= 2)
    place = jnp.where(valid, place, -1)
    keeps = {
        "all": None,
        "middle": ((zi >= 2) == (zo == 1)) | inner,
        "low": (zi <= 2) | inner,
        "high": (zi >= 1) | inner,
    }
    wide = dot(conv_ref[...], spread_cols).astype(BF16)
    for e in range(3):
        total = jnp.zeros((128, 256), F32)
        for ab in range(9):
            at = ((ab * 3 + e) * 2 + layer) * CH
            total = jnp.where(place == ab, dot(spread_rows, wide[at : at + CH]), total)
        total = total * 0.5
        for out, name in outs:
            part = total if keeps[name] is None else jnp.where(keeps[name], total, 0.0)
            out[:, e * 256 : (e + 1) * 256] = part.astype(BF16)


def silu_of_half(h):
    return h + h * jnp.tanh(h)


def across(column, width):
    return jnp.concatenate([column] * (width // INNER), axis=1)


def shifts(ref, row, value):
    lane = lax.broadcasted_iota(jnp.int32, (16, NX), 1)
    none = jnp.zeros_like(value)
    ref[0, row : row + 16, :] = jnp.where(lane == 0, none, pltpu.roll(value, 1, 1))
    ref[2, row : row + 16, :] = jnp.where(lane == NX - 1, none, pltpu.roll(value, NX - 1, 1))


def lift(slab_ref, x_ref, par_ref):
    for z in range(DEPTH):
        cells = jnp.concatenate([slab_ref[z].astype(F32)] * 4, axis=0)
        for block in range(4):
            rows = slice(block * 16, block * 16 + 16)
            value = silu_of_half(across(par_ref[0, rows], NX) * cells + across(par_ref[1, rows], NX))
            value = value.astype(BF16)
            x_ref[1, z * 64 + block * 16 : z * 64 + block * 16 + 16, :] = value
            shifts(x_ref, z * 64 + block * 16, value)


def shift_rows(x_ref, first, count):
    for block in range(count):
        row = first + block * 16
        shifts(x_ref, row, x_ref[1, row : row + 16, :])


CHUNK = 256


def convolve(w_ref, parts, bias, at):
    total = bias
    for e in range(3):
        cells = [ref[e, row : row + size, at : at + CHUNK] for ref, row, size in parts]
        cells = cells[0] if len(cells) == 1 else jnp.concatenate(cells, 0)
        total = total + dot(w_ref[:, e * 256 : (e + 1) * 256], cells)
    return silu_of_half(total)


def bias_of(par_ref, index):
    return across(jnp.concatenate([par_ref[index]] * 2, 0), CHUNK)


def prepare_kernel(
    at_ref, slab_ref, conv_ref, vector_ref, par_ref, w1_ref, w1m_ref, w2a_ref, w2b_ref, x1_ref, x2_ref
):
    channel = lax.broadcasted_iota(jnp.int32, (4 * CH, CH), 0) // 4
    mine = channel == lax.broadcasted_iota(jnp.int32, (4 * CH, CH), 1)
    for index in range(5):
        values = vector_ref[index : index + 1, :]
        column = jnp.sum(jnp.where(mine, values, 0.0), axis=1, keepdims=True)
        if index < 4:
            column = 0.5 * column
        par_ref[index] = jnp.broadcast_to(column, (4 * CH, INNER))
    inner = at_ref[0] > 0
    build_weights(inner, conv_ref, 0, ((w1_ref, "all"), (w1m_ref, "middle")))
    build_weights(inner, conv_ref, 1, ((w2a_ref, "low"), (w2b_ref, "high")))
    lift(slab_ref, x1_ref, par_ref)
    bias = bias_of(par_ref, 2)
    for at in range(0, NX, CHUNK):
        act = convolve(w1_ref, ((x1_ref, 0, 256),), bias, at)
        x2_ref[1, :, at : at + CHUNK] = act.astype(BF16)
    shift_rows(x2_ref, 0, 8)


def filter_kernel(
    left_ref, own_ref, par_ref, w1_ref, w1m_ref, w2a_ref, w2b_ref, x1_ref, x2_ref,
    full_ref, ends_ref, twiddle_ref, out_ref, x1, x2,
):
    lift(left_ref, x1, par_ref)
    bias = bias_of(par_ref, 2)
    for at in range(0, NX, CHUNK):
        act = convolve(w1_ref, ((x1, 0, 256),), bias, at)
        x2[1, :128, at : at + CHUNK] = act.astype(BF16)
        act = convolve(w1m_ref, ((x1, 128, 128), (x1_ref, 0, 128)), bias, at)
        x2[1, 128:, at : at + CHUNK] = act.astype(BF16)
    shift_rows(x2, 0, 16)
    bias = bias_of(par_ref, 3)
    mix = across(par_ref[4], CHUNK)
    a = []
    for at in range(0, NX, CHUNK):
        slices = []
        for w_ref, parts in (
            (w2a_ref, ((x2, 0, 256),)),
            (w2b_ref, ((x2, 128, 128), (x2_ref, 0, 128))),
        ):
            act = convolve(w_ref, parts, bias, at)
            for zo in range(2):
                terms = act[zo * 64 : zo * 64 + 64] * mix
                total = terms[0:8]
                for pair in range(1, 8):
                    total = total + terms[pair * 8 : pair * 8 + 8]
                z = 2 + len(slices)
                cells_ref = left_ref if z < DEPTH else own_ref
                base = cells_ref[z % DEPTH, :, at : at + CHUNK].astype(F32)
                slices.append(base + total[0:4] + total[4:8])
        mixed = jnp.concatenate([slices[z][y : y + 1] for y in range(NY) for z in range(DEPTH)], 0)
        a += [mixed[:, i : i + INNER] for i in range(0, CHUNK, INNER)]
    forward(a, full_ref, ends_ref, twiddle_ref, out_ref)


def cos16(n):
    return math.cos(2 * math.pi * (n % 16) / 16)


def sin16(n):
    return math.sin(2 * math.pi * (n % 16) / 16)


def weigh(terms):
    total = None
    for factor, value in terms:
        if abs(factor) < 1e-9:
            continue
        if abs(factor - 1) < 1e-9:
            term = value
        elif abs(factor + 1) < 1e-9:
            term = -value
        else:
            term = value * factor
        total = term if total is None else total + term
    return total


def forward(a, full_ref, ends_ref, twiddle_ref, out_ref):
    plus = [a[i] + a[16 - i] for i in range(1, 8)]
    minus = [a[i] - a[16 - i] for i in range(1, 8)]
    re, im = [], []
    for k1 in range(9):
        re.append(weigh([(1, a[0]), ((-1) ** k1, a[8])] + [(cos16(k1 * i), plus[i - 1]) for i in range(1, 8)]))
        im.append(weigh([(-sin16(k1 * i), minus[i - 1]) for i in range(1, 8)]))
    rows = []
    for k1 in range(1, 8):
        c, s = twiddle_ref[k1 - 1 : k1], twiddle_ref[k1 + 7 : k1 + 8]
        rows.append(jnp.concatenate([re[k1] * c + im[k1] * s, im[k1] * c - re[k1] * s], 1))
    whole = dot(jnp.concatenate(rows, 0).astype(BF16), full_ref[...])
    blocks = [
        dot(re[0].astype(BF16), ends_ref[:, :INNER]),
        dot(re[8].astype(BF16), ends_ref[:, INNER:]),
    ]
    for k1 in range(1, 8):
        for h in range(2):
            blocks.append(whole[(k1 - 1) * 16 : k1 * 16, h * INNER : (h + 1) * INNER])
    for y in range(NY):
        for b in range(BLOCKS):
            out_ref[RANK[y * BLOCKS + b]] = blocks[b][y * DEPTH : (y + 1) * DEPTH].astype(BF16)


def inverse_kernel(in_ref, full_ref, ends_ref, twiddle_ref, out_ref):
    blocks = [
        jnp.concatenate([in_ref[RANK[y * BLOCKS + b]].astype(F32) for y in range(NY)], 0).astype(BF16)
        for b in range(BLOCKS)
    ]
    even = dot(blocks[0], ends_ref[:, :INNER])
    mid = dot(blocks[1], ends_ref[:, INNER:])
    lows = jnp.concatenate([blocks[2 * k1] for k1 in range(1, 8)], 0)
    highs = jnp.concatenate([blocks[2 * k1 + 1] for k1 in range(1, 8)], 0)
    whole = dot(lows, full_ref[:INNER]) + dot(highs, full_ref[INNER:])
    re, im = [], []
    for k1 in range(1, 8):
        part = whole[(k1 - 1) * 16 : k1 * 16]
        b_re, b_im = part[:, :INNER], part[:, INNER:]
        c, s = twiddle_ref[k1 - 1 : k1], twiddle_ref[k1 + 7 : k1 + 8]
        re.append(b_re * c - b_im * s)
        im.append(b_re * s + b_im * c)
    scale = 1.0 / (NX * NZ)
    even, mid = even * scale, mid * scale
    re, im = [v * scale for v in re], [v * scale for v in im]
    out = [None] * RADIX
    for x1 in range(9):
        p = weigh([(1, even), ((-1) ** x1, mid)] + [(cos16(k1 * x1), re[k1 - 1]) for k1 in range(1, 8)])
        q = weigh([(sin16(k1 * x1), im[k1 - 1]) for k1 in range(1, 8)])
        if q is None:
            out[x1] = p
        else:
            out[x1], out[16 - x1] = p - q, p + q
    for x1 in range(RADIX):
        for z in range(DEPTH):
            rows = [out[x1][y * DEPTH + z : y * DEPTH + z + 1] for y in range(NY)]
            out_ref[z, :, x1 * INNER : (x1 + 1) * INNER] = jnp.concatenate(rows, 0)


def wedge_kernel(at_ref, wedge_ref, plus_ref, minus_ref):
    block = at_ref[0] % BLOCKS
    k = lax.broadcasted_iota(jnp.int32, (NX, INNER), 0)
    j = lax.broadcasted_iota(jnp.int32, (NX, INNER), 1)
    col = j % HALF
    k1 = jnp.where(block == 0, 0, jnp.where(block == 1, 8, block // 2))
    high = jnp.where(block < 2, 0, block % 2)
    mine = k1 + RADIX * (HALF * high + col)
    target = jnp.where(j < HALF, mine, (NX - mine) % NX)
    special = (block == 0) & (col == 0)
    quarter = special & (k == NX // 2)
    hit = (k == target)
    plain = jnp.where(hit, jnp.where(special, 0.25, 1.0), 0.0) + jnp.where(quarter, 0.25, 0.0)
    cross = jnp.where(special, jnp.where(hit, 0.25, 0.0) - jnp.where(quarter, 0.25, 0.0), 0.0)
    select = jnp.concatenate([plain, cross], 1).astype(BF16)
    whole = wedge_ref[...]
    top = whole.astype(BF16)
    rest = (whole - top.astype(F32)).astype(BF16)
    picked = dot(top, select) + dot(rest, select)
    r = lax.broadcasted_iota(jnp.int32, (NZ, NZ), 0)
    c = lax.broadcasted_iota(jnp.int32, (NZ, NZ), 1)
    flip = ((r + c) % NZ == 0).astype(F32).astype(BF16)
    top = picked.astype(BF16)
    rest = (picked - top.astype(F32)).astype(BF16)
    turned = dot(flip, top) + dot(flip, rest)
    low = lax.broadcasted_iota(jnp.int32, (NZ, INNER), 1) < HALF
    for out, at in ((plus_ref, 0), (minus_ref, INNER)):
        here, there = picked[:, at : at + INNER], turned[:, at : at + INNER]
        both = jnp.where(low, here + pltpu.roll(there, HALF, 1), there + pltpu.roll(here, HALF, 1))
        out[...] = both


def middle_kernel(own_ref, other_ref, plus_ref, minus_ref, ahead_ref, back_ref, out_ref):
    delta = (own_ref[...].astype(F32) - other_ref[...].astype(F32)).astype(BF16)
    sign = jnp.where(lax.broadcasted_iota(jnp.int32, (NZ, INNER), 1) < HALF, 1.0, -1.0)
    both = dot(ahead_ref[...], delta)
    cos_part, sin_part = both[:NZ], pltpu.roll(both[NZ:], HALF, 1)
    freq = cos_part + sign * sin_part
    mirror = sign * cos_part - sin_part
    weighted = (plus_ref[...] * freq + minus_ref[...] * mirror).astype(BF16)
    both = dot(back_ref[...], weighted)
    out_ref[...] = (both[:NZ] - sign * pltpu.roll(both[NZ:], HALF, 1)).astype(BF16)


def call(kernel, outs, *args, scratch=(), megabytes=8, smem=0, flops=10**7):
    many = isinstance(outs, list)
    spec = lambda space: pl.BlockSpec(memory_space=space)
    moved = sum(a.size * a.dtype.itemsize for a in args)
    return pl.pallas_call(
        kernel,
        out_shape=outs,
        in_specs=[spec(pltpu.SMEM)] * smem + [spec(pltpu.VMEM)] * (len(args) - smem),
        out_specs=[spec(pltpu.VMEM)] * len(outs) if many else spec(pltpu.VMEM),
        scratch_shapes=scratch,
        compiler_params=params(megabytes),
        cost_estimate=pl.CostEstimate(flops=flops, bytes_accessed=moved, transcendentals=0),
    )(*args)


def exchange(chunks):
    return lax.all_to_all(
        chunks, "gz", split_axis=0, concat_axis=0, tiled=True, axis_index_groups=[list(ORDER)]
    )


def shape(*dims, dtype=BF16):
    return jax.ShapeDtypeStruct(dims, dtype)


def body(
    density,
    lift_weight,
    lift_bias,
    conv_first,
    bias_first,
    conv_second,
    bias_second,
    projection,
    wedge,
):
    full_x, ends_x, full_i, ends_i, twiddle = x_tables()
    ahead, back = z_tables()
    place = lax.axis_index("gz")
    slab = density[0]
    rounded = slab.astype(BF16)
    left = lax.ppermute(rounded, "gz", [(i, (i + 1) % GZ) for i in range(GZ)])

    at = place.astype(jnp.int32).reshape(1)
    vectors = jnp.stack([lift_weight, lift_bias, bias_first, bias_second, projection])
    convs = jnp.concatenate([conv_first, conv_second], 0).transpose(2, 3, 4, 0, 1).reshape(54 * CH, CH)
    par, w1, w1m, w2a, w2b, x1, x2 = call(
        prepare_kernel,
        [shape(5, 4 * CH, INNER, dtype=F32)] + [shape(128, 768)] * 4 + [shape(3, 256, NX), shape(3, 128, NX)],
        at, rounded, convs, vectors, smem=1, megabytes=24, flops=10**9,
    )
    plus, minus = call(
        wedge_kernel, [shape(NZ, INNER, dtype=F32)] * 2, at, wedge, smem=1, megabytes=16, flops=10**9,
    )
    spectrum = call(
        filter_kernel, shape(GZ, DEPTH, INNER), left, slab, par, w1, w1m, w2a, w2b, x1, x2,
        full_x, ends_x, twiddle,
        scratch=[pltpu.VMEM((3, 256, NX), BF16), pltpu.VMEM((3, 256, NX), BF16)],
        megabytes=24, flops=10**9,
    )
    pencils = exchange(spectrum).reshape(NZ, INNER)
    other = lax.ppermute(pencils, "half", [(i, i ^ 1) for i in range(lax.axis_size("half"))])
    returned = call(
        middle_kernel, shape(NZ, INNER), pencils, other, plus, minus, ahead, back,
    )
    slabs = exchange(returned.reshape(GZ, DEPTH, INNER))
    residual = call(
        inverse_kernel, shape(DEPTH, NY, NX, dtype=F32), slabs, full_i, ends_i, twiddle,
    )
    return residual[None]


def solution(mesh):
    placed = (P("half", "gz", None, None), P(), P(), P(), P(), P(), P(), P(), P())
    return jax.shard_map(
        body, mesh=mesh, in_specs=placed, out_specs=P("half", "gz", None, None), check_vma=False
    )
```

```python
import math

import jax
import jax.numpy as jnp
import numpy as np
from jax import lax
from jax.experimental import pallas as pl
from jax.experimental.pallas import tpu as pltpu
from jax.sharding import PartitionSpec as P

NX, CH, NY, NZ = 2048, 16, 4, 256
GZ = 64
DEPTH = NZ // GZ
RADIX, INNER = 16, NX // 16
HALF = INNER // 2
BLOCKS = 16
LAG = 2
F32, BF16 = jnp.float32, jnp.bfloat16
FORTH = (
    34, 47, 16, 38, 36, 54, 4, 52, 51, 48, 45, 20, 7, 50, 30, 49,
    44, 15, 58, 35, 10, 9, 55, 25, 18, 11, 40, 42, 62, 41, 21, 23,
    2, 13, 3, 61, 56, 32, 43, 26, 31, 60, 6, 59, 29, 39, 14, 0,
    28, 17, 12, 46, 8, 22, 33, 24, 27, 19, 63, 1, 5, 53, 57, 37,
)
BACK = (
    42, 58, 26, 38, 46, 22, 62, 41, 10, 30, 34, 43, 54, 47, 50, 6,
    57, 25, 14, 27, 45, 37, 39, 59, 18, 53, 33, 29, 23, 11, 63, 2,
    35, 21, 40, 9, 31, 55, 61, 44, 49, 15, 56, 7, 24, 36, 13, 17,
    19, 5, 51, 32, 1, 3, 60, 52, 8, 28, 20, 4, 16, 48, 12, 0,
)
FORTH_RANK = tuple(FORTH.index(i) for i in range(GZ))
BACK_RANK = tuple(BACK.index(i) for i in range(GZ))


def dot(a, b):
    return jnp.dot(a, b, preferred_element_type=F32)


def params(megabytes=8):
    return pltpu.CompilerParams(vmem_limit_bytes=megabytes << 20)


def turn(product, size):
    angle = 2.0 * math.pi * (product % size) / size
    return np.cos(angle), np.sin(angle)


def x_tables():
    x0 = np.arange(INNER)[:, None]
    k0 = np.arange(INNER)[None, :]
    c, s = turn(x0 * k0, INNER)
    pick = lambda t, h: t[:, h * HALF : (h + 1) * HALF]
    from_re = np.concatenate([pick(c, 0), pick(-s, 0), pick(c, 1), pick(-s, 1)], 1)
    from_im = np.concatenate([pick(s, 0), pick(c, 0), pick(s, 1), pick(c, 1)], 1)
    full = np.concatenate([from_re, from_im], 0)
    first = np.concatenate([pick(c, 0), pick(-s, 0)], 1)
    first[:, HALF] = c[:, HALF]
    c8, s8 = turn(x0 * (1 + 2 * np.arange(HALF)[None, :]), 2 * INNER)
    middle = np.concatenate([c8, -s8], 1)
    k1 = np.arange(1, 8)[:, None]
    ct, st = turn(k1 * np.arange(INNER)[None, :], NX)
    twiddle = np.concatenate([ct, np.zeros((1, INNER)), st, np.zeros((1, INNER))], 0)
    return (
        full.astype(jnp.bfloat16),
        np.concatenate([first, middle], 1).astype(jnp.bfloat16),
        full.T.astype(jnp.bfloat16),
        np.concatenate([first.T, middle.T], 1).astype(jnp.bfloat16),
        twiddle.astype(np.float32),
    )


def z_tables():
    kz = np.arange(NZ)
    slices = lambda order: (DEPTH * np.array(order)[:, None] + np.arange(DEPTH)[None, :]).reshape(NZ)
    ahead = np.concatenate(turn(kz[:, None] * (slices(FORTH) - LAG)[None, :], NZ), 0)
    back = np.concatenate(turn(slices(BACK)[:, None] * kz[None, :], NZ), 0)
    return ahead.astype(jnp.bfloat16), back.astype(jnp.bfloat16)


def build_weights(inner, conv_ref, layer, outs):
    rows = lax.broadcasted_iota(jnp.int32, (128, 256), 0)
    cols = lax.broadcasted_iota(jnp.int32, (128, 256), 1)
    zo, yo = rows // 64, rows % 4
    zi, yi = cols // 64, cols % 4
    spread_rows = (
        lax.broadcasted_iota(jnp.int32, (128, CH), 0) % 64 // 4
        == lax.broadcasted_iota(jnp.int32, (128, CH), 1)
    ).astype(F32).astype(BF16)
    spread_cols = (
        lax.broadcasted_iota(jnp.int32, (CH, 256), 1) % 64 // 4
        == lax.broadcasted_iota(jnp.int32, (CH, 256), 0)
    ).astype(F32).astype(BF16)
    place = (zi - zo) * 3 + (yi - yo + 1)
    valid = (yi - yo + 1 >= 0) & (yi - yo + 1 <= 2) & (zi - zo >= 0) & (zi - zo <= 2)
    place = jnp.where(valid, place, -1)
    keeps = {
        "all": None,
        "middle": ((zi >= 2) == (zo == 1)) | inner,
        "low": (zi <= 2) | inner,
        "high": (zi >= 1) | inner,
    }
    wide = dot(conv_ref[...], spread_cols).astype(BF16)
    for e in range(3):
        total = jnp.zeros((128, 256), F32)
        for ab in range(9):
            at = ((ab * 3 + e) * 2 + layer) * CH
            total = jnp.where(place == ab, dot(spread_rows, wide[at : at + CH]), total)
        total = total * 0.5
        for out, name in outs:
            part = total if keeps[name] is None else jnp.where(keeps[name], total, 0.0)
            out[:, e * 256 : (e + 1) * 256] = part.astype(BF16)


def silu_of_half(h):
    return h + h * jnp.tanh(h)


def across(column, width):
    return jnp.concatenate([column] * (width // INNER), axis=1)


def shifts(ref, row, value):
    lane = lax.broadcasted_iota(jnp.int32, (16, NX), 1)
    none = jnp.zeros_like(value)
    ref[0, row : row + 16, :] = jnp.where(lane == 0, none, pltpu.roll(value, 1, 1))
    ref[2, row : row + 16, :] = jnp.where(lane == NX - 1, none, pltpu.roll(value, NX - 1, 1))


def lift(slab_ref, x_ref, par_ref):
    for z in range(DEPTH):
        cells = jnp.concatenate([slab_ref[z].astype(F32)] * 4, axis=0)
        for block in range(4):
            rows = slice(block * 16, block * 16 + 16)
            value = silu_of_half(across(par_ref[0, rows], NX) * cells + across(par_ref[1, rows], NX))
            value = value.astype(BF16)
            x_ref[1, z * 64 + block * 16 : z * 64 + block * 16 + 16, :] = value
            shifts(x_ref, z * 64 + block * 16, value)


def shift_rows(x_ref, first, count):
    for block in range(count):
        row = first + block * 16
        shifts(x_ref, row, x_ref[1, row : row + 16, :])


CHUNK = 256


def convolve(w_ref, parts, bias, at):
    total = bias
    for e in range(3):
        cells = [ref[e, row : row + size, at : at + CHUNK] for ref, row, size in parts]
        cells = cells[0] if len(cells) == 1 else jnp.concatenate(cells, 0)
        total = total + dot(w_ref[:, e * 256 : (e + 1) * 256], cells)
    return silu_of_half(total)


def bias_of(par_ref, index):
    return across(jnp.concatenate([par_ref[index]] * 2, 0), CHUNK)


def prepare_kernel(
    at_ref, slab_ref, conv_ref, vector_ref, par_ref, w1_ref, w1m_ref, w2a_ref, w2b_ref, x1_ref, x2_ref
):
    channel = lax.broadcasted_iota(jnp.int32, (4 * CH, CH), 0) // 4
    mine = channel == lax.broadcasted_iota(jnp.int32, (4 * CH, CH), 1)
    for index in range(5):
        values = vector_ref[index : index + 1, :]
        column = jnp.sum(jnp.where(mine, values, 0.0), axis=1, keepdims=True)
        if index < 4:
            column = 0.5 * column
        par_ref[index] = jnp.broadcast_to(column, (4 * CH, INNER))
    inner = at_ref[0] > 0
    build_weights(inner, conv_ref, 0, ((w1_ref, "all"), (w1m_ref, "middle")))
    build_weights(inner, conv_ref, 1, ((w2a_ref, "low"), (w2b_ref, "high")))
    lift(slab_ref, x1_ref, par_ref)
    bias = bias_of(par_ref, 2)
    for at in range(0, NX, CHUNK):
        act = convolve(w1_ref, ((x1_ref, 0, 256),), bias, at)
        x2_ref[1, :, at : at + CHUNK] = act.astype(BF16)
    shift_rows(x2_ref, 0, 8)


def filter_kernel(
    left_ref, own_ref, par_ref, w1_ref, w1m_ref, w2a_ref, w2b_ref, x1_ref, x2_ref,
    full_ref, ends_ref, twiddle_ref, out_ref, x1, x2,
):
    lift(left_ref, x1, par_ref)
    bias = bias_of(par_ref, 2)
    for at in range(0, NX, CHUNK):
        act = convolve(w1_ref, ((x1, 0, 256),), bias, at)
        x2[1, :128, at : at + CHUNK] = act.astype(BF16)
        act = convolve(w1m_ref, ((x1, 128, 128), (x1_ref, 0, 128)), bias, at)
        x2[1, 128:, at : at + CHUNK] = act.astype(BF16)
    shift_rows(x2, 0, 16)
    bias = bias_of(par_ref, 3)
    mix = across(par_ref[4], CHUNK)
    a = []
    for at in range(0, NX, CHUNK):
        slices = []
        for w_ref, parts in (
            (w2a_ref, ((x2, 0, 256),)),
            (w2b_ref, ((x2, 128, 128), (x2_ref, 0, 128))),
        ):
            act = convolve(w_ref, parts, bias, at)
            for zo in range(2):
                terms = act[zo * 64 : zo * 64 + 64] * mix
                total = terms[0:8]
                for pair in range(1, 8):
                    total = total + terms[pair * 8 : pair * 8 + 8]
                z = 2 + len(slices)
                cells_ref = left_ref if z < DEPTH else own_ref
                base = cells_ref[z % DEPTH, :, at : at + CHUNK].astype(F32)
                slices.append(base + total[0:4] + total[4:8])
        mixed = jnp.concatenate([slices[z][y : y + 1] for y in range(NY) for z in range(DEPTH)], 0)
        a += [mixed[:, i : i + INNER] for i in range(0, CHUNK, INNER)]
    forward(a, full_ref, ends_ref, twiddle_ref, out_ref)


def cos16(n):
    return math.cos(2 * math.pi * (n % 16) / 16)


def sin16(n):
    return math.sin(2 * math.pi * (n % 16) / 16)


def weigh(terms):
    total = None
    for factor, value in terms:
        if abs(factor) < 1e-9:
            continue
        if abs(factor - 1) < 1e-9:
            term = value
        elif abs(factor + 1) < 1e-9:
            term = -value
        else:
            term = value * factor
        total = term if total is None else total + term
    return total


def forward(a, full_ref, ends_ref, twiddle_ref, out_ref):
    plus = [a[i] + a[16 - i] for i in range(1, 8)]
    minus = [a[i] - a[16 - i] for i in range(1, 8)]
    re, im = [], []
    for k1 in range(9):
        re.append(weigh([(1, a[0]), ((-1) ** k1, a[8])] + [(cos16(k1 * i), plus[i - 1]) for i in range(1, 8)]))
        im.append(weigh([(-sin16(k1 * i), minus[i - 1]) for i in range(1, 8)]))
    rows = []
    for k1 in range(1, 8):
        c, s = twiddle_ref[k1 - 1 : k1], twiddle_ref[k1 + 7 : k1 + 8]
        rows.append(jnp.concatenate([re[k1] * c + im[k1] * s, im[k1] * c - re[k1] * s], 1))
    whole = dot(jnp.concatenate(rows, 0).astype(BF16), full_ref[...])
    blocks = [
        dot(re[0].astype(BF16), ends_ref[:, :INNER]),
        dot(re[8].astype(BF16), ends_ref[:, INNER:]),
    ]
    for k1 in range(1, 8):
        for h in range(2):
            blocks.append(whole[(k1 - 1) * 16 : k1 * 16, h * INNER : (h + 1) * INNER])
    for y in range(NY):
        for b in range(BLOCKS):
            out_ref[FORTH_RANK[y * BLOCKS + b]] = blocks[b][y * DEPTH : (y + 1) * DEPTH].astype(BF16)


def inverse_kernel(in_ref, full_ref, ends_ref, twiddle_ref, out_ref):
    blocks = [
        jnp.concatenate([in_ref[BACK_RANK[y * BLOCKS + b]].astype(F32) for y in range(NY)], 0).astype(BF16)
        for b in range(BLOCKS)
    ]
    even = dot(blocks[0], ends_ref[:, :INNER])
    mid = dot(blocks[1], ends_ref[:, INNER:])
    lows = jnp.concatenate([blocks[2 * k1] for k1 in range(1, 8)], 0)
    highs = jnp.concatenate([blocks[2 * k1 + 1] for k1 in range(1, 8)], 0)
    whole = dot(lows, full_ref[:INNER]) + dot(highs, full_ref[INNER:])
    re, im = [], []
    for k1 in range(1, 8):
        part = whole[(k1 - 1) * 16 : k1 * 16]
        b_re, b_im = part[:, :INNER], part[:, INNER:]
        c, s = twiddle_ref[k1 - 1 : k1], twiddle_ref[k1 + 7 : k1 + 8]
        re.append(b_re * c - b_im * s)
        im.append(b_re * s + b_im * c)
    scale = 1.0 / (NX * NZ)
    even, mid = even * scale, mid * scale
    re, im = [v * scale for v in re], [v * scale for v in im]
    out = [None] * RADIX
    for x1 in range(9):
        p = weigh([(1, even), ((-1) ** x1, mid)] + [(cos16(k1 * x1), re[k1 - 1]) for k1 in range(1, 8)])
        q = weigh([(sin16(k1 * x1), im[k1 - 1]) for k1 in range(1, 8)])
        if q is None:
            out[x1] = p
        else:
            out[x1], out[16 - x1] = p - q, p + q
    for x1 in range(RADIX):
        for z in range(DEPTH):
            rows = [out[x1][y * DEPTH + z : y * DEPTH + z + 1] for y in range(NY)]
            out_ref[z, :, x1 * INNER : (x1 + 1) * INNER] = jnp.concatenate(rows, 0)


def wedge_kernel(at_ref, wedge_ref, plus_ref, minus_ref):
    block = at_ref[0] % BLOCKS
    k = lax.broadcasted_iota(jnp.int32, (NX, INNER), 0)
    j = lax.broadcasted_iota(jnp.int32, (NX, INNER), 1)
    col = j % HALF
    k1 = jnp.where(block == 0, 0, jnp.where(block == 1, 8, block // 2))
    high = jnp.where(block < 2, 0, block % 2)
    mine = k1 + RADIX * (HALF * high + col)
    target = jnp.where(j < HALF, mine, (NX - mine) % NX)
    special = (block == 0) & (col == 0)
    quarter = special & (k == NX // 2)
    hit = (k == target)
    plain = jnp.where(hit, jnp.where(special, 0.25, 1.0), 0.0) + jnp.where(quarter, 0.25, 0.0)
    cross = jnp.where(special, jnp.where(hit, 0.25, 0.0) - jnp.where(quarter, 0.25, 0.0), 0.0)
    select = jnp.concatenate([plain, cross], 1).astype(BF16)
    whole = wedge_ref[...]
    top = whole.astype(BF16)
    rest = (whole - top.astype(F32)).astype(BF16)
    picked = dot(top, select) + dot(rest, select)
    r = lax.broadcasted_iota(jnp.int32, (NZ, NZ), 0)
    c = lax.broadcasted_iota(jnp.int32, (NZ, NZ), 1)
    flip = ((r + c) % NZ == 0).astype(F32).astype(BF16)
    top = picked.astype(BF16)
    rest = (picked - top.astype(F32)).astype(BF16)
    turned = dot(flip, top) + dot(flip, rest)
    low = lax.broadcasted_iota(jnp.int32, (NZ, INNER), 1) < HALF
    for out, at in ((plus_ref, 0), (minus_ref, INNER)):
        here, there = picked[:, at : at + INNER], turned[:, at : at + INNER]
        both = jnp.where(low, here + pltpu.roll(there, HALF, 1), there + pltpu.roll(here, HALF, 1))
        out[...] = both


def middle_kernel(own_ref, other_ref, plus_ref, minus_ref, ahead_ref, back_ref, out_ref):
    delta = (own_ref[...].astype(F32) - other_ref[...].astype(F32)).astype(BF16)
    sign = jnp.where(lax.broadcasted_iota(jnp.int32, (NZ, INNER), 1) < HALF, 1.0, -1.0)
    both = dot(ahead_ref[...], delta)
    cos_part, sin_part = both[:NZ], pltpu.roll(both[NZ:], HALF, 1)
    freq = cos_part + sign * sin_part
    mirror = sign * cos_part - sin_part
    weighted = (plus_ref[...] * freq + minus_ref[...] * mirror).astype(BF16)
    both = dot(back_ref[...], weighted)
    out_ref[...] = (both[:NZ] - sign * pltpu.roll(both[NZ:], HALF, 1)).astype(BF16)


def call(kernel, outs, *args, scratch=(), megabytes=8, smem=0, flops=10**7):
    many = isinstance(outs, list)
    spec = lambda space: pl.BlockSpec(memory_space=space)
    moved = sum(a.size * a.dtype.itemsize for a in args)
    return pl.pallas_call(
        kernel,
        out_shape=outs,
        in_specs=[spec(pltpu.SMEM)] * smem + [spec(pltpu.VMEM)] * (len(args) - smem),
        out_specs=[spec(pltpu.VMEM)] * len(outs) if many else spec(pltpu.VMEM),
        scratch_shapes=scratch,
        compiler_params=params(megabytes),
        cost_estimate=pl.CostEstimate(flops=flops, bytes_accessed=moved, transcendentals=0),
    )(*args)


def exchange(chunks, order):
    return lax.all_to_all(
        chunks, "gz", split_axis=0, concat_axis=0, tiled=True, axis_index_groups=[list(order)]
    )


def shape(*dims, dtype=BF16):
    return jax.ShapeDtypeStruct(dims, dtype)


def body(
    density,
    lift_weight,
    lift_bias,
    conv_first,
    bias_first,
    conv_second,
    bias_second,
    projection,
    wedge,
):
    full_x, ends_x, full_i, ends_i, twiddle = x_tables()
    ahead, back = z_tables()
    place = lax.axis_index("gz")
    slab = density[0]
    rounded = slab.astype(BF16)
    left = lax.ppermute(rounded, "gz", [(i, (i + 1) % GZ) for i in range(GZ)])

    at = place.astype(jnp.int32).reshape(1)
    vectors = jnp.stack([lift_weight, lift_bias, bias_first, bias_second, projection])
    convs = jnp.concatenate([conv_first, conv_second], 0).transpose(2, 3, 4, 0, 1).reshape(54 * CH, CH)
    par, w1, w1m, w2a, w2b, x1, x2 = call(
        prepare_kernel,
        [shape(5, 4 * CH, INNER, dtype=F32)] + [shape(128, 768)] * 4 + [shape(3, 256, NX), shape(3, 128, NX)],
        at, rounded, convs, vectors, smem=1, megabytes=24, flops=10**9,
    )
    plus, minus = call(
        wedge_kernel, [shape(NZ, INNER, dtype=F32)] * 2, at, wedge, smem=1, megabytes=16, flops=10**9,
    )
    spectrum = call(
        filter_kernel, shape(GZ, DEPTH, INNER), left, slab, par, w1, w1m, w2a, w2b, x1, x2,
        full_x, ends_x, twiddle,
        scratch=[pltpu.VMEM((3, 256, NX), BF16), pltpu.VMEM((3, 256, NX), BF16)],
        megabytes=24, flops=10**9,
    )
    pencils = exchange(spectrum, FORTH).reshape(NZ, INNER)
    other = lax.ppermute(pencils, "half", [(i, i ^ 1) for i in range(lax.axis_size("half"))])
    returned = call(
        middle_kernel, shape(NZ, INNER), pencils, other, plus, minus, ahead, back,
    )
    slabs = exchange(returned.reshape(GZ, DEPTH, INNER), BACK)
    residual = call(
        inverse_kernel, shape(DEPTH, NY, NX, dtype=F32), slabs, full_i, ends_i, twiddle,
    )
    return residual[None]


def solution(mesh):
    placed = (P("half", "gz", None, None), P(), P(), P(), P(), P(), P(), P(), P())
    return jax.shard_map(
        body, mesh=mesh, in_specs=placed, out_specs=P("half", "gz", None, None), check_vma=False
    )
```

```python
import math

import jax
import jax.numpy as jnp
import numpy as np
from jax import lax
from jax.experimental import pallas as pl
from jax.experimental.pallas import tpu as pltpu
from jax.sharding import PartitionSpec as P

NX, CH, NY, NZ = 2048, 16, 4, 256
GZ = 64
DEPTH = NZ // GZ
RADIX, INNER = 16, NX // 16
HALF = INNER // 2
BLOCKS = 16
LAG = 2
F32, BF16 = jnp.float32, jnp.bfloat16
FORTH = (
    34, 47, 16, 38, 36, 54, 4, 52, 51, 48, 45, 20, 7, 50, 30, 49,
    44, 15, 58, 35, 10, 9, 55, 25, 18, 11, 40, 42, 62, 41, 21, 23,
    2, 13, 3, 61, 56, 32, 43, 26, 31, 60, 6, 59, 29, 39, 14, 0,
    28, 17, 12, 46, 8, 22, 33, 24, 27, 19, 63, 1, 5, 53, 57, 37,
)
BACK = (
    42, 58, 26, 38, 46, 22, 62, 41, 10, 30, 34, 43, 54, 47, 50, 6,
    57, 25, 14, 27, 45, 37, 39, 59, 18, 53, 33, 29, 23, 11, 63, 2,
    35, 21, 40, 9, 31, 55, 61, 44, 49, 15, 56, 7, 24, 36, 13, 17,
    19, 5, 51, 32, 1, 3, 60, 52, 8, 28, 20, 4, 16, 48, 12, 0,
)
FORTH_RANK = tuple(FORTH.index(i) for i in range(GZ))
BACK_RANK = tuple(BACK.index(i) for i in range(GZ))


def dot(a, b):
    return jnp.dot(a, b, preferred_element_type=F32)


def params(megabytes=8):
    return pltpu.CompilerParams(vmem_limit_bytes=megabytes << 20)


def turn(product, size):
    angle = 2.0 * math.pi * (product % size) / size
    return np.cos(angle), np.sin(angle)


def x_tables():
    x0 = np.arange(INNER)[:, None]
    k0 = np.arange(INNER)[None, :]
    c, s = turn(x0 * k0, INNER)
    pick = lambda t, h: t[:, h * HALF : (h + 1) * HALF]
    from_re = np.concatenate([pick(c, 0), pick(-s, 0), pick(c, 1), pick(-s, 1)], 1)
    from_im = np.concatenate([pick(s, 0), pick(c, 0), pick(s, 1), pick(c, 1)], 1)
    full = np.concatenate([from_re, from_im], 0)
    first = np.concatenate([pick(c, 0), pick(-s, 0)], 1)
    first[:, HALF] = c[:, HALF]
    c8, s8 = turn(x0 * (1 + 2 * np.arange(HALF)[None, :]), 2 * INNER)
    middle = np.concatenate([c8, -s8], 1)
    k1 = np.arange(1, 8)[:, None]
    ct, st = turn(k1 * np.arange(INNER)[None, :], NX)
    twiddle = np.concatenate([ct, np.zeros((1, INNER)), st, np.zeros((1, INNER))], 0)
    return (
        full.astype(jnp.bfloat16),
        np.concatenate([first, middle], 1).astype(jnp.bfloat16),
        full.T.astype(jnp.bfloat16),
        np.concatenate([first.T, middle.T], 1).astype(jnp.bfloat16),
        twiddle.astype(np.float32),
    )


def z_tables():
    kz = np.arange(NZ)
    slices = lambda order: (DEPTH * np.array(order)[:, None] + np.arange(DEPTH)[None, :]).reshape(NZ)
    ahead = np.concatenate(turn(kz[:, None] * (slices(FORTH) - LAG)[None, :], NZ), 0)
    back = np.concatenate(turn(slices(BACK)[:, None] * kz[None, :], NZ), 0)
    return ahead.astype(jnp.bfloat16), back.astype(jnp.bfloat16)


def build_weights(inner, conv_ref, layer, outs):
    rows = lax.broadcasted_iota(jnp.int32, (128, 256), 0)
    cols = lax.broadcasted_iota(jnp.int32, (128, 256), 1)
    zo, yo = rows // 64, rows % 4
    zi, yi = cols // 64, cols % 4
    spread_rows = (
        lax.broadcasted_iota(jnp.int32, (128, CH), 0) % 64 // 4
        == lax.broadcasted_iota(jnp.int32, (128, CH), 1)
    ).astype(F32).astype(BF16)
    spread_cols = (
        lax.broadcasted_iota(jnp.int32, (CH, 256), 1) % 64 // 4
        == lax.broadcasted_iota(jnp.int32, (CH, 256), 0)
    ).astype(F32).astype(BF16)
    place = (zi - zo) * 3 + (yi - yo + 1)
    valid = (yi - yo + 1 >= 0) & (yi - yo + 1 <= 2) & (zi - zo >= 0) & (zi - zo <= 2)
    place = jnp.where(valid, place, -1)
    keeps = {
        "all": None,
        "middle": ((zi >= 2) == (zo == 1)) | inner,
        "low": (zi <= 2) | inner,
        "high": (zi >= 1) | inner,
    }
    wide = dot(conv_ref[...], spread_cols).astype(BF16)
    for e in range(3):
        total = jnp.zeros((128, 256), F32)
        for ab in range(9):
            at = ((ab * 3 + e) * 2 + layer) * CH
            total = jnp.where(place == ab, dot(spread_rows, wide[at : at + CH]), total)
        total = total * 0.5
        for out, name in outs:
            part = total if keeps[name] is None else jnp.where(keeps[name], total, 0.0)
            out[:, e * 256 : (e + 1) * 256] = part.astype(BF16)


def silu_of_half(h):
    return h + h * jnp.tanh(h)


def across(column, width):
    return jnp.concatenate([column] * (width // INNER), axis=1)


def shifts(ref, row, value):
    lane = lax.broadcasted_iota(jnp.int32, (16, NX), 1)
    none = jnp.zeros_like(value)
    ref[0, row : row + 16, :] = jnp.where(lane == 0, none, pltpu.roll(value, 1, 1))
    ref[2, row : row + 16, :] = jnp.where(lane == NX - 1, none, pltpu.roll(value, NX - 1, 1))


def lift(slab_ref, x_ref, par_ref):
    for z in range(DEPTH):
        cells = jnp.concatenate([slab_ref[z].astype(F32)] * 4, axis=0)
        for block in range(4):
            rows = slice(block * 16, block * 16 + 16)
            value = silu_of_half(across(par_ref[0, rows], NX) * cells + across(par_ref[1, rows], NX))
            value = value.astype(BF16)
            x_ref[1, z * 64 + block * 16 : z * 64 + block * 16 + 16, :] = value
            shifts(x_ref, z * 64 + block * 16, value)


def shift_rows(x_ref, first, count):
    for block in range(count):
        row = first + block * 16
        shifts(x_ref, row, x_ref[1, row : row + 16, :])


CHUNK = 512


def convolve(w_ref, parts, bias, at):
    total = bias
    for e in range(3):
        cells = [ref[e, row : row + size, at : at + CHUNK] for ref, row, size in parts]
        cells = cells[0] if len(cells) == 1 else jnp.concatenate(cells, 0)
        total = total + dot(w_ref[:, e * 256 : (e + 1) * 256], cells)
    return silu_of_half(total)


def bias_of(par_ref, index):
    return across(jnp.concatenate([par_ref[index]] * 2, 0), CHUNK)


def prepare_kernel(
    at_ref, slab_ref, conv_ref, vector_ref, par_ref, w1_ref, w1m_ref, w2a_ref, w2b_ref, x1_ref, x2_ref
):
    channel = lax.broadcasted_iota(jnp.int32, (4 * CH, CH), 0) // 4
    mine = channel == lax.broadcasted_iota(jnp.int32, (4 * CH, CH), 1)
    for index in range(5):
        values = vector_ref[index : index + 1, :]
        column = jnp.sum(jnp.where(mine, values, 0.0), axis=1, keepdims=True)
        if index < 4:
            column = 0.5 * column
        par_ref[index] = jnp.broadcast_to(column, (4 * CH, INNER))
    inner = at_ref[0] > 0
    build_weights(inner, conv_ref, 0, ((w1_ref, "all"), (w1m_ref, "middle")))
    build_weights(inner, conv_ref, 1, ((w2a_ref, "low"), (w2b_ref, "high")))
    lift(slab_ref, x1_ref, par_ref)
    bias = bias_of(par_ref, 2)
    for at in range(0, NX, CHUNK):
        act = convolve(w1_ref, ((x1_ref, 0, 256),), bias, at)
        x2_ref[1, :, at : at + CHUNK] = act.astype(BF16)
    shift_rows(x2_ref, 0, 8)


def filter_kernel(
    left_ref, own_ref, par_ref, w1_ref, w1m_ref, w2a_ref, w2b_ref, x1_ref, x2_ref,
    full_ref, ends_ref, twiddle_ref, out_ref, x1, x2,
):
    lift(left_ref, x1, par_ref)
    bias = bias_of(par_ref, 2)
    for at in range(0, NX, CHUNK):
        act = convolve(w1_ref, ((x1, 0, 256),), bias, at)
        x2[1, :128, at : at + CHUNK] = act.astype(BF16)
        act = convolve(w1m_ref, ((x1, 128, 128), (x1_ref, 0, 128)), bias, at)
        x2[1, 128:, at : at + CHUNK] = act.astype(BF16)
    shift_rows(x2, 0, 16)
    bias = bias_of(par_ref, 3)
    mix = across(par_ref[4], CHUNK)
    a = []
    for at in range(0, NX, CHUNK):
        slices = []
        for w_ref, parts in (
            (w2a_ref, ((x2, 0, 256),)),
            (w2b_ref, ((x2, 128, 128), (x2_ref, 0, 128))),
        ):
            act = convolve(w_ref, parts, bias, at)
            for zo in range(2):
                terms = act[zo * 64 : zo * 64 + 64] * mix
                total = terms[0:8]
                for pair in range(1, 8):
                    total = total + terms[pair * 8 : pair * 8 + 8]
                z = 2 + len(slices)
                cells_ref = left_ref if z < DEPTH else own_ref
                base = cells_ref[z % DEPTH, :, at : at + CHUNK].astype(F32)
                slices.append(base + total[0:4] + total[4:8])
        mixed = jnp.concatenate([slices[z][y : y + 1] for y in range(NY) for z in range(DEPTH)], 0)
        a += [mixed[:, i : i + INNER] for i in range(0, CHUNK, INNER)]
    forward(a, full_ref, ends_ref, twiddle_ref, out_ref)


def cos16(n):
    return math.cos(2 * math.pi * (n % 16) / 16)


def sin16(n):
    return math.sin(2 * math.pi * (n % 16) / 16)


def weigh(terms):
    total = None
    for factor, value in terms:
        if abs(factor) < 1e-9:
            continue
        if abs(factor - 1) < 1e-9:
            term = value
        elif abs(factor + 1) < 1e-9:
            term = -value
        else:
            term = value * factor
        total = term if total is None else total + term
    return total


def forward(a, full_ref, ends_ref, twiddle_ref, out_ref):
    plus = [a[i] + a[16 - i] for i in range(1, 8)]
    minus = [a[i] - a[16 - i] for i in range(1, 8)]
    re, im = [], []
    for k1 in range(9):
        re.append(weigh([(1, a[0]), ((-1) ** k1, a[8])] + [(cos16(k1 * i), plus[i - 1]) for i in range(1, 8)]))
        im.append(weigh([(-sin16(k1 * i), minus[i - 1]) for i in range(1, 8)]))
    rows = []
    for k1 in range(1, 8):
        c, s = twiddle_ref[k1 - 1 : k1], twiddle_ref[k1 + 7 : k1 + 8]
        rows.append(jnp.concatenate([re[k1] * c + im[k1] * s, im[k1] * c - re[k1] * s], 1))
    whole = dot(jnp.concatenate(rows, 0).astype(BF16), full_ref[...])
    blocks = [
        dot(re[0].astype(BF16), ends_ref[:, :INNER]),
        dot(re[8].astype(BF16), ends_ref[:, INNER:]),
    ]
    for k1 in range(1, 8):
        for h in range(2):
            blocks.append(whole[(k1 - 1) * 16 : k1 * 16, h * INNER : (h + 1) * INNER])
    for y in range(NY):
        for b in range(BLOCKS):
            out_ref[FORTH_RANK[y * BLOCKS + b]] = blocks[b][y * DEPTH : (y + 1) * DEPTH].astype(BF16)


def inverse_kernel(in_ref, full_ref, ends_ref, twiddle_ref, out_ref):
    blocks = [
        jnp.concatenate([in_ref[BACK_RANK[y * BLOCKS + b]].astype(F32) for y in range(NY)], 0).astype(BF16)
        for b in range(BLOCKS)
    ]
    even = dot(blocks[0], ends_ref[:, :INNER])
    mid = dot(blocks[1], ends_ref[:, INNER:])
    lows = jnp.concatenate([blocks[2 * k1] for k1 in range(1, 8)], 0)
    highs = jnp.concatenate([blocks[2 * k1 + 1] for k1 in range(1, 8)], 0)
    whole = dot(lows, full_ref[:INNER]) + dot(highs, full_ref[INNER:])
    re, im = [], []
    for k1 in range(1, 8):
        part = whole[(k1 - 1) * 16 : k1 * 16]
        b_re, b_im = part[:, :INNER], part[:, INNER:]
        c, s = twiddle_ref[k1 - 1 : k1], twiddle_ref[k1 + 7 : k1 + 8]
        re.append(b_re * c - b_im * s)
        im.append(b_re * s + b_im * c)
    scale = 1.0 / (NX * NZ)
    even, mid = even * scale, mid * scale
    re, im = [v * scale for v in re], [v * scale for v in im]
    out = [None] * RADIX
    for x1 in range(9):
        p = weigh([(1, even), ((-1) ** x1, mid)] + [(cos16(k1 * x1), re[k1 - 1]) for k1 in range(1, 8)])
        q = weigh([(sin16(k1 * x1), im[k1 - 1]) for k1 in range(1, 8)])
        if q is None:
            out[x1] = p
        else:
            out[x1], out[16 - x1] = p - q, p + q
    for x1 in range(RADIX):
        for z in range(DEPTH):
            rows = [out[x1][y * DEPTH + z : y * DEPTH + z + 1] for y in range(NY)]
            out_ref[z, :, x1 * INNER : (x1 + 1) * INNER] = jnp.concatenate(rows, 0)


def wedge_kernel(at_ref, wedge_ref, plus_ref, minus_ref):
    block = at_ref[0] % BLOCKS
    k = lax.broadcasted_iota(jnp.int32, (NX, INNER), 0)
    j = lax.broadcasted_iota(jnp.int32, (NX, INNER), 1)
    col = j % HALF
    k1 = jnp.where(block == 0, 0, jnp.where(block == 1, 8, block // 2))
    high = jnp.where(block < 2, 0, block % 2)
    mine = k1 + RADIX * (HALF * high + col)
    target = jnp.where(j < HALF, mine, (NX - mine) % NX)
    special = (block == 0) & (col == 0)
    quarter = special & (k == NX // 2)
    hit = (k == target)
    plain = jnp.where(hit, jnp.where(special, 0.25, 1.0), 0.0) + jnp.where(quarter, 0.25, 0.0)
    cross = jnp.where(special, jnp.where(hit, 0.25, 0.0) - jnp.where(quarter, 0.25, 0.0), 0.0)
    select = jnp.concatenate([plain, cross], 1).astype(BF16)
    whole = wedge_ref[...]
    top = whole.astype(BF16)
    rest = (whole - top.astype(F32)).astype(BF16)
    picked = dot(top, select) + dot(rest, select)
    r = lax.broadcasted_iota(jnp.int32, (NZ, NZ), 0)
    c = lax.broadcasted_iota(jnp.int32, (NZ, NZ), 1)
    flip = ((r + c) % NZ == 0).astype(F32).astype(BF16)
    top = picked.astype(BF16)
    rest = (picked - top.astype(F32)).astype(BF16)
    turned = dot(flip, top) + dot(flip, rest)
    low = lax.broadcasted_iota(jnp.int32, (NZ, INNER), 1) < HALF
    for out, at in ((plus_ref, 0), (minus_ref, INNER)):
        here, there = picked[:, at : at + INNER], turned[:, at : at + INNER]
        both = jnp.where(low, here + pltpu.roll(there, HALF, 1), there + pltpu.roll(here, HALF, 1))
        out[...] = both


def middle_kernel(own_ref, other_ref, plus_ref, minus_ref, ahead_ref, back_ref, out_ref):
    delta = (own_ref[...].astype(F32) - other_ref[...].astype(F32)).astype(BF16)
    sign = jnp.where(lax.broadcasted_iota(jnp.int32, (NZ, INNER), 1) < HALF, 1.0, -1.0)
    both = dot(ahead_ref[...], delta)
    cos_part, sin_part = both[:NZ], pltpu.roll(both[NZ:], HALF, 1)
    freq = cos_part + sign * sin_part
    mirror = sign * cos_part - sin_part
    weighted = (plus_ref[...] * freq + minus_ref[...] * mirror).astype(BF16)
    both = dot(back_ref[...], weighted)
    out_ref[...] = (both[:NZ] - sign * pltpu.roll(both[NZ:], HALF, 1)).astype(BF16)


def call(kernel, outs, *args, scratch=(), megabytes=8, smem=0, flops=10**7):
    many = isinstance(outs, list)
    spec = lambda space: pl.BlockSpec(memory_space=space)
    moved = sum(a.size * a.dtype.itemsize for a in args)
    return pl.pallas_call(
        kernel,
        out_shape=outs,
        in_specs=[spec(pltpu.SMEM)] * smem + [spec(pltpu.VMEM)] * (len(args) - smem),
        out_specs=[spec(pltpu.VMEM)] * len(outs) if many else spec(pltpu.VMEM),
        scratch_shapes=scratch,
        compiler_params=params(megabytes),
        cost_estimate=pl.CostEstimate(flops=flops, bytes_accessed=moved, transcendentals=0),
    )(*args)


def exchange(chunks, order):
    return lax.all_to_all(
        chunks, "gz", split_axis=0, concat_axis=0, tiled=True, axis_index_groups=[list(order)]
    )


def shape(*dims, dtype=BF16):
    return jax.ShapeDtypeStruct(dims, dtype)


def body(
    density,
    lift_weight,
    lift_bias,
    conv_first,
    bias_first,
    conv_second,
    bias_second,
    projection,
    wedge,
):
    full_x, ends_x, full_i, ends_i, twiddle = x_tables()
    ahead, back = z_tables()
    place = lax.axis_index("gz")
    slab = density[0]
    rounded = slab.astype(BF16)
    left = lax.ppermute(rounded, "gz", [(i, (i + 1) % GZ) for i in range(GZ)])

    at = place.astype(jnp.int32).reshape(1)
    vectors = jnp.stack([lift_weight, lift_bias, bias_first, bias_second, projection])
    convs = jnp.concatenate([conv_first, conv_second], 0).transpose(2, 3, 4, 0, 1).reshape(54 * CH, CH)
    par, w1, w1m, w2a, w2b, x1, x2 = call(
        prepare_kernel,
        [shape(5, 4 * CH, INNER, dtype=F32)] + [shape(128, 768)] * 4 + [shape(3, 256, NX), shape(3, 128, NX)],
        at, rounded, convs, vectors, smem=1, megabytes=24, flops=10**9,
    )
    plus, minus = call(
        wedge_kernel, [shape(NZ, INNER, dtype=F32)] * 2, at, wedge, smem=1, megabytes=16, flops=10**9,
    )
    spectrum = call(
        filter_kernel, shape(GZ, DEPTH, INNER), left, slab, par, w1, w1m, w2a, w2b, x1, x2,
        full_x, ends_x, twiddle,
        scratch=[pltpu.VMEM((3, 256, NX), BF16), pltpu.VMEM((3, 256, NX), BF16)],
        megabytes=24, flops=10**9,
    )
    pencils = exchange(spectrum, FORTH).reshape(NZ, INNER)
    other = lax.ppermute(pencils, "half", [(i, i ^ 1) for i in range(lax.axis_size("half"))])
    returned = call(
        middle_kernel, shape(NZ, INNER), pencils, other, plus, minus, ahead, back,
    )
    slabs = exchange(returned.reshape(GZ, DEPTH, INNER), BACK)
    residual = call(
        inverse_kernel, shape(DEPTH, NY, NX, dtype=F32), slabs, full_i, ends_i, twiddle,
    )
    return residual[None]


def solution(mesh):
    placed = (P("half", "gz", None, None), P(), P(), P(), P(), P(), P(), P(), P())
    return jax.shard_map(
        body, mesh=mesh, in_specs=placed, out_specs=P("half", "gz", None, None), check_vma=False
    )
```
